32 devices in a mesh: segment: 4 (over y, core), dp: 2 (over x), expert: 4 (over z).
Axes of the slice: x: 2, y: 2, z: 4, core: 2. Of those that a mesh axis runs over, the one named last changes fastest.
Arguments:
- saved_b: bfloat16 [4, 1024, 2048], P('segment', ('dp', 'expert')), may hold values from -6 to 6
- route_b: int32 [4, 1024, 1], P('segment', ('dp', 'expert')), may hold values from 0 to 3; in each aligned block of 128 rows (0 to 127, 128 to 255, ..., all dimensions but the last counted through in order) at most 40 rows name the same one
- gate_b: float32 [4, 1024, 1], P('segment', ('dp', 'expert')), may hold values from 0.2 to 1
- grad_y_b: bfloat16 [4, 1024, 2048], P('segment', ('dp', 'expert')), may hold values from -6 to 6
- w_in: bfloat16 [4, 4, 2048, 768], P('segment', 'expert'), may hold values from -0.125 to 0.125
- w_out: bfloat16 [4, 4, 768, 2048], P('segment', 'expert'), may hold values from -0.21875 to 0.21875
Outputs:
- grad_x_b: bfloat16 [4, 1024, 2048], P('segment', ('dp', 'expert'))
- grad_in: bfloat16 [4, 4, 2048, 768], P('segment', 'expert', None, 'dp')
The draws below stay inside these ranges and needn't reach their ends.
Inputs may be any that keep to these rules, and one draw needn't show every extreme that they name: `route_b`: of the 128 tokens of one device of a section, at most 40 pick any one expert; some device sends exactly 40 to some expert.
All inputs are finite; a program needn't handle non-finite values.
Results may differ from the reference program's by a relative error of at most 0.01.
Values may be sent and summed in bfloat16 or wider, within the bound.
A program may use at most 64 MiB of HBM per device.

```python
import math
import jax
import jax.numpy as jnp
import numpy as np
from jax import lax

D = 2048
F = 768
TOK_DEV = 128
N_EXP_ALL = 4
CAP = 40
TOKENS = 1024
N_SEGMENT = 4
N_DP = 2
N_EXPERT = 4


def levels(rng, shape, cuts, low, high):
    gain, own = 1.0, jax.random.fold_in(rng, 6)
    for dim, parts in cuts:
        draws = jnp.exp(jax.random.uniform(jax.random.fold_in(own, dim), (parts,), jnp.float32, low / len(cuts), high / len(cuts)))
        gain = gain * jnp.repeat(draws, shape[dim] // parts).reshape([-1 if axis == dim else 1 for axis in range(len(shape))])
    return gain


def shared_out(own_key, own, number, rows, number_of, top, most, slope):
    ranking = jax.random.permutation(own_key, number_of)
    heavy_load, ordinary = portions_of(number_of, rows * top, most, slope, True), portions_of(number_of, rows * top, most, slope, False)
    places = jnp.arange(number_of)

    def named(sizes, rotation):
        used = int((sizes > 0).sum())
        fixed = max(1, used // 4)
        passed = fixed + (places - fixed + rotation * (used - fixed)) % max(1, number_of - fixed)
        return jnp.zeros((number_of,), jnp.int32).at[ranking[jnp.where(places < fixed, places, passed)]].set(jnp.asarray(sizes, jnp.int32))

    sizes = jnp.where(number % 4 == 0, named(heavy_load, number // 4), named(ordinary, number - number // 4 - 1))
    mixed = jax.random.permutation(jax.random.fold_in(own, 3), number_of)
    source_of, sink = mixed[0:number_of // 2 * 2:2], mixed[1:number_of // 2 * 2:2]
    room = jnp.minimum(sizes[source_of] - 1, most - sizes[sink]) // 2
    room = jnp.where((source_of == ranking[0]) | (sink == ranking[0]) | (sizes[sink] == 0), 0, jnp.maximum(room, 0))
    passed = jax.random.randint(jax.random.fold_in(own, 4), (number_of // 2,), 0, 1 << 20) % (room + 1)
    sizes = sizes.at[source_of].add(-passed).at[sink].add(passed)
    labels = jnp.searchsorted(jnp.cumsum(sizes), jnp.arange(rows * top), side="right").astype(jnp.int32)
    table = labels.reshape(top, rows).T
    table = table[jax.random.permutation(jax.random.fold_in(own, 1), rows)]
    rotation = jax.random.randint(jax.random.fold_in(own, 2), (rows, 1), 0, top)
    return jnp.take_along_axis(table, (jnp.arange(top)[None, :] + rotation) % top, axis=1)


def portions_of(number_of, total, bound, skew, full):
    loads = [(1 << 20) // math.isqrt(grade ** skew) + 1 for grade in range(1, number_of + 1)]
    largest = bound if full else min(bound, max(-(-total // number_of), total * loads[0] // sum(loads)))
    least = 1 if total - largest >= number_of - 1 else 0
    given, rest = [largest] + [least] * (number_of - 1), total - largest - least * (number_of - 1)
    while rest > 0:
        candidates = [i for i in range(1, number_of) if given[i] < largest] or [i for i in range(1, number_of) if given[i] < bound]
        whole, left = sum([loads[i] for i in candidates]), rest
        for i in candidates:
            more = min(bound - given[i], max(1, left * loads[i] // whole), rest)
            given[i] = given[i] + more
            rest = rest - more
    return np.array(given)


def bell_draw(rng, shape, spread, reach, cuts=(), kind=jnp.bfloat16):
    entries = spread * jax.random.normal(rng, shape, jnp.float32)
    if cuts:
        entries = entries * levels(rng, shape, cuts, -0.22, 0.18)
    return jnp.clip(entries, -reach, reach).astype(kind)


def setup_inputs(seed: int = 0) -> dict:
    seeds = jax.random.split(jax.random.key(seed), 7)
    saved_b = bell_draw(seeds[0], (N_SEGMENT, TOKENS, D), 1.0, 6.0, ((0, 4), (1, 8)))
    route_b_keys = jax.random.split(jax.random.fold_in(seeds[1], 1), N_SEGMENT * TOKENS // TOK_DEV)
    route_b_turns = jax.random.permutation(jax.random.fold_in(seeds[1], 3), N_SEGMENT * TOKENS // TOK_DEV)
    route_b = jax.vmap(lambda own, number: shared_out(jax.random.fold_in(seeds[1], 2), own, number, TOK_DEV, N_EXPERT, 1, CAP, 2))(route_b_keys, route_b_turns).reshape((N_SEGMENT, TOKENS, 1))
    gate_b = jnp.clip(0.2 + 0.8 * jax.random.uniform(seeds[2], (N_SEGMENT, TOKENS, 1), jnp.float32) ** levels(seeds[2], (N_SEGMENT, TOKENS, 1), ((0, 4), (1, 8)), -0.2, 0.2), 0.2, 1.0)
    grad_y_b = bell_draw(seeds[3], (N_SEGMENT, TOKENS, D), 1.0, 6.0, ((0, 4), (1, 8)))
    w_in = bell_draw(seeds[4], (N_SEGMENT, N_EXP_ALL, D, F), D ** -0.5, 0.125, ((0, 4), (1, 4)))
    w_out = bell_draw(seeds[5], (N_SEGMENT, N_EXP_ALL, F, D), F ** -0.5, 0.21875, ((0, 4), (1, 4)))
    return {"saved_b": saved_b, "route_b": route_b, "gate_b": gate_b, "grad_y_b": grad_y_b, "w_in": w_in, "w_out": w_out}


def silu_grad(value):
    sigma = jax.nn.sigmoid(value)
    return sigma * (1.0 + value * (1.0 - sigma))

def positions(route):
    expert_ids = route[..., 0]
    onehot = (expert_ids[..., None] == jnp.arange(N_EXPERT, dtype=jnp.int32)).astype(jnp.int32)
    before = jnp.cumsum(onehot, axis=1) - onehot
    return (expert_ids * CAP + lax.optimization_barrier(jnp.sum(before * onehot, axis=2))).astype(jnp.int32)

def fill_one(buffer, position, values):
    return buffer.at[position].set(values)

def read_one(buffer, position):
    return buffer[position]

def to_slots(values, position):
    devices = values.shape[0]
    empty = jnp.zeros((devices, N_EXPERT * CAP, D), values.dtype)
    filled = jax.vmap(fill_one)(empty, position, values)
    return filled.reshape(devices, N_EXPERT, CAP, D).transpose(1, 0, 2, 3).reshape(N_EXPERT, devices * CAP, D)

def from_slots(rows, position):
    devices = position.shape[0]
    grouped = rows.reshape(N_EXPERT, devices, CAP, D).transpose(1, 0, 2, 3).reshape(devices, N_EXPERT * CAP, D)
    return jax.vmap(read_one)(grouped, position)

def section(pack):
    saved_b, route_b, gate_b, cotangent, w_in, w_out = pack
    devices = N_DP * N_EXPERT
    shape_rows = (devices, TOK_DEV, D)
    weight_in = w_in.astype(jnp.float32)
    weight_out = w_out.astype(jnp.float32)
    scaled = (gate_b.reshape(devices, TOK_DEV, 1) * cotangent.reshape(shape_rows).astype(jnp.float32)).astype(jnp.bfloat16)
    pos_b = positions(route_b.reshape(devices, TOK_DEV, 1))
    slots_x = to_slots(saved_b.reshape(shape_rows), pos_b).astype(jnp.float32)
    slots_g = to_slots(scaled, pos_b).astype(jnp.float32)
    pre_b = jnp.einsum('erd,edf->erf', slots_x, weight_in)
    grad_h = jnp.einsum('erd,efd->erf', slots_g, weight_out)
    grad_pre = (grad_h * silu_grad(pre_b)).astype(jnp.bfloat16)
    grad_slots = jnp.einsum('erf,edf->erd', grad_pre.astype(jnp.float32), weight_in).astype(jnp.bfloat16)
    grad_x = from_slots(grad_slots, pos_b)
    group_rows = N_EXPERT * CAP
    group_x = slots_x.reshape(N_EXPERT, N_DP, group_rows, D)
    group_pre = grad_pre.astype(jnp.float32).reshape(N_EXPERT, N_DP, group_rows, F)
    part_in = jnp.einsum('egrd,egrf->egdf', group_x, group_pre).astype(jnp.bfloat16)
    part_in = lax.optimization_barrier(part_in)
    grad_in = lax.optimization_barrier(jnp.sum(part_in.astype(jnp.float32), axis=1)).astype(jnp.bfloat16)
    return (grad_x.reshape(TOKENS, D), grad_in)

def reference(saved_b, route_b, gate_b, grad_y_b, w_in, w_out):
    arrived = jnp.roll(grad_y_b, -1, axis=0)
    results = lax.map(section, (saved_b, route_b, gate_b, arrived, w_in, w_out))
    return (results[0], results[1])
```

```python
import functools
import jax
import jax.numpy as jnp
from jax import lax
from jax.experimental import pallas as pl
from jax.experimental.pallas import tpu as pltpu
from jax.sharding import PartitionSpec as P

F32 = jnp.float32
BF16 = jnp.bfloat16


def kernel(
    sizes,
    route_ref, gate_ref, saved_hbm, gy_hbm, win_hbm, wout_hbm,
    gx_hbm, gin_hbm,
    saved_v, cot, win_v, wout_v, send_x, send_g, x_all, g_all, dsilu,
    gp_send, gp_all, ret, back, acc, gx_v, gin_v,
    loc, seg_s, seg_r, xs, xr, gs, gr, fs, fr, ps, pr, bs, br, outs,
):
    n_seg, n_dp, n_exp, cap, chunks = sizes
    me_s, me_d, me_z = lax.axis_index("segment"), lax.axis_index("dp"), lax.axis_index("expert")
    tok, width = saved_v.shape
    hidden = win_v.shape[1]
    part = hidden // n_dp
    step = width // chunks

    def turn(i):
        return 1 + lax.rem(i + n_exp // 2 - 2, n_exp - 1)

    def to_of(i):
        return lax.rem(me_z + turn(i), n_exp)

    def from_of(i):
        return lax.rem(me_z + n_exp - turn(i), n_exp)

    def remote(src, dst, ss, rs, seg=None, dp=None, exp=None):
        dev = (
            me_s if seg is None else seg,
            me_d if dp is None else dp,
            me_z if exp is None else exp,
        )
        return pltpu.make_async_remote_copy(
            src_ref=src, dst_ref=dst, send_sem=ss, recv_sem=rs,
            device_id=dev, device_id_type=pl.DeviceIdType.MESH,
        )

    in_saved = pltpu.make_async_copy(saved_hbm.at[0], saved_v, loc.at[0])
    in_win = pltpu.make_async_copy(win_hbm.at[0, 0], win_v, loc.at[1])
    in_wout = pltpu.make_async_copy(wout_hbm.at[0, 0], wout_v, loc.at[2])
    in_saved.start()

    before_s = lax.rem(me_s + n_seg - 1, n_seg)
    after_s = lax.rem(me_s + 1, n_seg)
    barrier = pltpu.get_barrier_semaphore()
    peers = [(before_s, me_d, me_z), (after_s, me_d, me_z)]
    peers += [(me_s, lax.rem(me_d + d, n_dp), me_z) for d in range(1, n_dp)]
    peers += [(me_s, me_d, lax.rem(me_z + k, n_exp)) for k in range(1, n_exp)]
    for peer in peers:
        pl.semaphore_signal(barrier, inc=1, device_id=peer, device_id_type=pl.DeviceIdType.MESH)

    rows_t = lax.broadcasted_iota(jnp.int32, (tok, tok), 0)
    cols_t = lax.broadcasted_iota(jnp.int32, (tok, tok), 1)
    route = jnp.sum(jnp.where(rows_t == cols_t, route_ref[...], 0), axis=1, keepdims=True)
    gate = jnp.sum(jnp.where(rows_t == cols_t, gate_ref[...], 0.0), axis=1, keepdims=True)
    lanes = lax.broadcasted_iota(jnp.int32, (tok, 128), 1)
    onehot = (route == lanes).astype(F32)
    lower = (cols_t < rows_t).astype(BF16)
    ahead = jnp.dot(lower, onehot.astype(BF16), preferred_element_type=F32)
    rank = jnp.sum(ahead * onehot, axis=1, keepdims=True).astype(jnp.int32)
    pos_col = route * cap + rank
    pos_row = jnp.sum(jnp.where(rows_t == cols_t, pos_col, 0), axis=0, keepdims=True)

    def table(expert):
        slots = lax.broadcasted_iota(jnp.int32, (cap, tok), 0) + expert * cap
        return (slots == pos_row).astype(F32).astype(BF16)

    def table_t(expert):
        slots = lax.broadcasted_iota(jnp.int32, (tok, cap), 1) + expert * cap
        return (slots == pos_col).astype(F32).astype(BF16)

    pl.semaphore_wait(barrier, len(peers))
    seg_copy = remote(gy_hbm.at[0], cot, seg_s.at[0], seg_r.at[0], seg=before_s)
    seg_copy.start()
    in_saved.wait()
    saved = saved_v[...]

    def x_copy(i):
        return remote(send_x.at[i - 1], x_all.at[me_d, me_z], xs.at[i - 1], xr.at[me_z], exp=to_of(i))

    for i in range(1, n_exp):
        send_x[i - 1] = jnp.dot(table(to_of(i)), saved, preferred_element_type=F32).astype(BF16)
        x_copy(i).start()
    in_win.start()
    in_wout.start()
    x_all[me_d, me_z] = jnp.dot(table(me_z), saved, preferred_element_type=F32).astype(BF16)

    def forward(d, block):
        return remote(
            x_all.at[me_d, block], x_all.at[me_d, block],
            fs.at[d - 1, block], fr.at[me_d, block], dp=lax.rem(me_d + d, n_dp),
        )

    for d in range(1, n_dp):
        forward(d, me_z).start()

    seg_copy.wait_recv()
    scaled = (gate * cot[...].astype(F32)).astype(BF16)

    def g_copy(i):
        return remote(send_g.at[i - 1], g_all.at[me_z], gs.at[i - 1], gr.at[me_z], exp=to_of(i))

    for i in range(1, n_exp):
        send_g[i - 1] = jnp.dot(table(to_of(i)), scaled, preferred_element_type=F32).astype(BF16)
        g_copy(i).start()
    g_all[me_z] = jnp.dot(table(me_z), scaled, preferred_element_type=F32).astype(BF16)

    for i in range(1, n_exp):
        block = from_of(i)
        remote(send_x.at[i - 1], x_all.at[me_d, block], xs.at[i - 1], xr.at[block], exp=block).wait_recv()
        for d in range(1, n_dp):
            forward(d, block).start()

    in_win.wait()
    own_x = x_all[me_d].astype(F32).reshape(n_exp * cap, width).astype(BF16)
    pre = jnp.dot(own_x, win_v[...], preferred_element_type=F32)
    sigma = jax.nn.sigmoid(pre)
    dsilu[...] = (sigma * (1.0 + pre * (1.0 - sigma))).reshape(n_exp, cap, hidden)
    in_wout.wait()

    def expert_block(block):
        grad_h = lax.dot_general(
            g_all[block], wout_v[...], (((1,), (1,)), ((), ())), preferred_element_type=F32
        )
        grad_pre = (grad_h * dsilu[block]).astype(BF16)
        for j in range(n_dp):
            gp_send[j, block] = grad_pre[:, j * part:(j + 1) * part]
        return lax.dot_general(
            grad_pre, win_v[...], (((1,), (1,)), ((), ())), preferred_element_type=F32
        ).astype(BF16)

    def b_copy(i, block):
        return remote(ret.at[i - 1], back.at[me_z], bs.at[i - 1], br.at[me_z], exp=block)

    back[me_z] = expert_block(me_z)

    def one_block(i, carry):
        block = from_of(i)
        remote(send_g.at[i - 1], g_all.at[block], gs.at[i - 1], gr.at[block], exp=block).wait_recv()
        ret[i - 1] = expert_block(block)
        b_copy(i, block).start()
        return carry

    lax.fori_loop(1, n_exp, one_block, 0)

    def p_copy(d):
        other = lax.rem(me_d + d, n_dp)
        return remote(gp_send.at[other], gp_all.at[me_d], ps.at[d - 1], pr.at[me_d], dp=other)

    for d in range(1, n_dp):
        p_copy(d).start()
    gp_all[me_d] = gp_send[me_d]
    acc[...] = jnp.dot(table_t(me_z), back[me_z], preferred_element_type=F32)

    for d in range(1, n_dp):
        other = lax.rem(me_d + n_dp - d, n_dp)
        for block in range(n_exp):
            remote(
                x_all.at[other, block], x_all.at[other, block],
                fs.at[d - 1, block], fr.at[other, block], dp=other,
            ).wait_recv()
        remote(gp_send.at[other], gp_all.at[other], ps.at[d - 1], pr.at[other], dp=other).wait_recv()

    all_gp = gp_all[...].astype(F32).reshape(n_dp * n_exp * cap, part).astype(BF16)

    def out_copy(c):
        rows = pl.ds(pl.multiple_of(c * step, step), step)
        return pltpu.make_async_copy(gin_v.at[rows], gin_hbm.at[rows], outs.at[c])

    def one_chunk(c, carry):
        at = pl.ds(pl.multiple_of(c * step, step), step)
        xs_c = x_all[:, :, :, at].astype(F32).reshape(n_dp * n_exp * cap, step).astype(BF16)
        gin_v[at, :] = lax.dot_general(
            xs_c, all_gp, (((0,), (0,)), ((), ())), preferred_element_type=F32
        ).astype(BF16)
        out_copy(c).start()
        return carry

    lax.fori_loop(0, chunks, one_chunk, 0)

    for i in range(1, n_exp):
        block = from_of(i)
        remote(ret.at[i - 1], back.at[block], bs.at[i - 1], br.at[block], exp=block).wait_recv()
        acc[...] += jnp.dot(table_t(block), back[block], preferred_element_type=F32)
    gx_v[...] = acc[...].astype(BF16)
    out_x = pltpu.make_async_copy(gx_v, gx_hbm, loc.at[3])
    out_x.start()

    seg_copy.wait_send()
    for i in range(1, n_exp):
        x_copy(i).wait_send()
        g_copy(i).wait_send()
        b_copy(i, from_of(i)).wait_send()
    for d in range(1, n_dp):
        for block in range(n_exp):
            forward(d, block).wait_send()
        p_copy(d).wait_send()
    for c in range(chunks):
        out_copy(c).wait()
    out_x.wait()


def body(saved_b, route_b, gate_b, grad_y_b, w_in, w_out):
    n_seg, n_dp, n_exp = lax.axis_size("segment"), lax.axis_size("dp"), lax.axis_size("expert")
    tok, width = saved_b.shape[1], saved_b.shape[2]
    hidden = w_in.shape[3]
    part = hidden // n_dp
    most = max(2, tok * 5 // (4 * n_exp))
    cap = -(-most // 8) * 8
    chunks = 4
    vmem = pl.BlockSpec(memory_space=pltpu.VMEM)
    hbm = pl.BlockSpec(memory_space=pl.ANY)
    dma = pltpu.SemaphoreType.DMA
    flops = 8 * n_exp * cap * width * hidden
    grad_x, grad_in = pl.pallas_call(
        functools.partial(kernel, (n_seg, n_dp, n_exp, cap, chunks)),
        out_shape=(
            jax.ShapeDtypeStruct((tok, width), BF16),
            jax.ShapeDtypeStruct((width, part), BF16),
        ),
        in_specs=[vmem, vmem, hbm, hbm, hbm, hbm],
        out_specs=(hbm, hbm),
        scratch_shapes=[
            pltpu.VMEM((tok, width), BF16),
            pltpu.VMEM((tok, width), BF16),
            pltpu.VMEM((width, hidden), BF16),
            pltpu.VMEM((hidden, width), BF16),
            pltpu.VMEM((n_exp - 1, cap, width), BF16),
            pltpu.VMEM((n_exp - 1, cap, width), BF16),
            pltpu.VMEM((n_dp, n_exp, cap, width), BF16),
            pltpu.VMEM((n_exp, cap, width), BF16),
            pltpu.VMEM((n_exp, cap, hidden), F32),
            pltpu.VMEM((n_dp, n_exp, cap, part), BF16),
            pltpu.VMEM((n_dp, n_exp, cap, part), BF16),
            pltpu.VMEM((n_exp - 1, cap, width), BF16),
            pltpu.VMEM((n_exp, cap, width), BF16),
            pltpu.VMEM((tok, width), F32),
            pltpu.VMEM((tok, width), BF16),
            pltpu.VMEM((width, part), BF16),
            dma((4,)),
            dma((1,)), dma((1,)),
            dma((n_exp,)), dma((n_exp,)),
            dma((n_exp,)), dma((n_exp,)),
            dma((n_dp, n_exp)), dma((n_dp, n_exp)),
            dma((n_dp,)), dma((n_dp,)),
            dma((n_exp,)), dma((n_exp,)),
            dma((chunks,)),
        ],
        compiler_params=pltpu.CompilerParams(
            collective_id=0, has_side_effects=True, vmem_limit_bytes=56 * 1024 * 1024
        ),
        cost_estimate=pl.CostEstimate(flops=flops, bytes_accessed=10 * 1024 * 1024, transcendentals=0),
    )(route_b.reshape(1, tok), gate_b.reshape(1, tok), saved_b, grad_y_b, w_in, w_out)
    return (grad_x[None], grad_in[None, None])


def solution(mesh):
    return jax.shard_map(
        body,
        mesh=mesh,
        in_specs=(
            P("segment", ("dp", "expert"), None),
            P("segment", ("dp", "expert"), None),
            P("segment", ("dp", "expert"), None),
            P("segment", ("dp", "expert"), None),
            P("segment", "expert", None, None),
            P("segment", "expert", None, None),
        ),
        out_specs=(P("segment", ("dp", "expert"), None), P("segment", "expert", None, "dp")),
        check_vma=False,
    )
```

```python
import functools
import jax
import jax.numpy as jnp
from jax import lax
from jax.experimental import pallas as pl
from jax.experimental.pallas import tpu as pltpu
from jax.sharding import PartitionSpec as P

F32 = jnp.float32
BF16 = jnp.bfloat16


def kernel(
    sizes,
    route_ref, gate_ref, saved_hbm, gy_hbm, win_hbm, wout_hbm,
    gx_hbm, gin_hbm,
    saved_v, cot, win_v, wout_v, send_x, send_g, x_all, g_all, dsilu,
    gp_send, gp_all, ret, back, acc, gx_v, gin_v,
    loc, seg_s, seg_r, xs, xr, gs, gr, fs, fr, ps, pr, bs, br, outs,
):
    n_seg, n_dp, n_exp, cap, chunks = sizes
    me_s, me_d, me_z = lax.axis_index("segment"), lax.axis_index("dp"), lax.axis_index("expert")
    tok, width = saved_v.shape
    hidden = win_v.shape[1]
    part = hidden // n_dp
    step = width // chunks

    paired = n_exp & (n_exp - 1) == 0

    def flip(k):
        other, bit = me_z, 1
        while bit < n_exp:
            other = other + bit * (k // bit % 2) * (1 - 2 * (me_z // bit % 2))
            bit *= 2
        return other

    def to_of(k):
        return flip(k) if paired else lax.rem(me_z + k, n_exp)

    def from_of(k):
        return flip(k) if paired else lax.rem(me_z + n_exp - k, n_exp)

    near_first = list(range(1, n_exp))
    far_first = near_first[n_exp // 2 - 1:] + near_first[:n_exp // 2 - 1]

    def remote(src, dst, ss, rs, seg=None, dp=None, exp=None):
        dev = (
            me_s if seg is None else seg,
            me_d if dp is None else dp,
            me_z if exp is None else exp,
        )
        return pltpu.make_async_remote_copy(
            src_ref=src, dst_ref=dst, send_sem=ss, recv_sem=rs,
            device_id=dev, device_id_type=pl.DeviceIdType.MESH,
        )

    in_saved = pltpu.make_async_copy(saved_hbm.at[0], saved_v, loc.at[0])
    in_win = pltpu.make_async_copy(win_hbm.at[0, 0], win_v, loc.at[1])
    in_wout = pltpu.make_async_copy(wout_hbm.at[0, 0], wout_v, loc.at[2])
    in_saved.start()

    before_s = lax.rem(me_s + n_seg - 1, n_seg)
    after_s = lax.rem(me_s + 1, n_seg)
    barrier = pltpu.get_barrier_semaphore()
    peers = [(before_s, me_d, me_z), (after_s, me_d, me_z)]
    peers += [(me_s, lax.rem(me_d + d, n_dp), me_z) for d in range(1, n_dp)]
    peers += [(me_s, me_d, lax.rem(me_z + k, n_exp)) for k in range(1, n_exp)]
    for peer in peers:
        pl.semaphore_signal(barrier, inc=1, device_id=peer, device_id_type=pl.DeviceIdType.MESH)

    rows_t = lax.broadcasted_iota(jnp.int32, (tok, tok), 0)
    cols_t = lax.broadcasted_iota(jnp.int32, (tok, tok), 1)
    route = jnp.sum(jnp.where(rows_t == cols_t, route_ref[...], 0), axis=1, keepdims=True)
    gate = jnp.sum(jnp.where(rows_t == cols_t, gate_ref[...], 0.0), axis=1, keepdims=True)
    lanes = lax.broadcasted_iota(jnp.int32, (tok, 128), 1)
    onehot = (route == lanes).astype(F32)
    lower = (cols_t < rows_t).astype(BF16)
    ahead = jnp.dot(lower, onehot.astype(BF16), preferred_element_type=F32)
    rank = jnp.sum(ahead * onehot, axis=1, keepdims=True).astype(jnp.int32)
    pos_col = route * cap + rank
    pos_row = jnp.sum(jnp.where(rows_t == cols_t, pos_col, 0), axis=0, keepdims=True)

    def table(expert):
        slots = lax.broadcasted_iota(jnp.int32, (cap, tok), 0) + expert * cap
        return (slots == pos_row).astype(F32).astype(BF16)

    def table_t(expert):
        slots = lax.broadcasted_iota(jnp.int32, (tok, cap), 1) + expert * cap
        return (slots == pos_col).astype(F32).astype(BF16)

    pl.semaphore_wait(barrier, len(peers))
    seg_copy = remote(gy_hbm.at[0], cot, seg_s.at[0], seg_r.at[0], seg=before_s)
    seg_copy.start()
    in_saved.wait()
    saved = saved_v[...]

    def x_copy(i):
        return remote(send_x.at[i - 1], x_all.at[me_d, me_z], xs.at[i - 1], xr.at[me_z], exp=to_of(i))

    for i in far_first:
        send_x[i - 1] = jnp.dot(table(to_of(i)), saved, preferred_element_type=F32).astype(BF16)
        x_copy(i).start()
    in_win.start()
    in_wout.start()
    x_all[me_d, me_z] = jnp.dot(table(me_z), saved, preferred_element_type=F32).astype(BF16)

    def forward(d, block):
        return remote(
            x_all.at[me_d, block], x_all.at[me_d, block],
            fs.at[d - 1, block], fr.at[me_d, block], dp=lax.rem(me_d + d, n_dp),
        )

    for d in range(1, n_dp):
        forward(d, me_z).start()

    seg_copy.wait_recv()
    scaled = (gate * cot[...].astype(F32)).astype(BF16)

    def g_copy(i):
        return remote(send_g.at[i - 1], g_all.at[me_z], gs.at[i - 1], gr.at[me_z], exp=to_of(i))

    for i in range(1, n_exp):
        send_g[i - 1] = jnp.dot(table(to_of(i)), scaled, preferred_element_type=F32).astype(BF16)
        g_copy(i).start()
    g_all[me_z] = jnp.dot(table(me_z), scaled, preferred_element_type=F32).astype(BF16)

    for i in range(1, n_exp):
        block = from_of(i)
        remote(send_x.at[i - 1], x_all.at[me_d, block], xs.at[i - 1], xr.at[block], exp=block).wait_recv()
        for d in range(1, n_dp):
            forward(d, block).start()

    in_win.wait()
    own_x = x_all[me_d].astype(F32).reshape(n_exp * cap, width).astype(BF16)
    pre = jnp.dot(own_x, win_v[...], preferred_element_type=F32)
    sigma = jax.nn.sigmoid(pre)
    dsilu[...] = (sigma * (1.0 + pre * (1.0 - sigma))).reshape(n_exp, cap, hidden)
    in_wout.wait()

    def expert_block(block):
        grad_h = lax.dot_general(
            g_all[block], wout_v[...], (((1,), (1,)), ((), ())), preferred_element_type=F32
        )
        grad_pre = (grad_h * dsilu[block]).astype(BF16)
        for j in range(n_dp):
            gp_send[j, block] = grad_pre[:, j * part:(j + 1) * part]
        return lax.dot_general(
            grad_pre, win_v[...], (((1,), (1,)), ((), ())), preferred_element_type=F32
        ).astype(BF16)

    def b_copy(i, block):
        return remote(ret.at[i - 1], back.at[me_z], bs.at[i - 1], br.at[me_z], exp=block)

    back[me_z] = expert_block(me_z)

    def one_block(i, carry):
        block = from_of(i)
        remote(send_g.at[i - 1], g_all.at[block], gs.at[i - 1], gr.at[block], exp=block).wait_recv()
        ret[i - 1] = expert_block(block)
        b_copy(i, block).start()
        return carry

    lax.fori_loop(1, n_exp, one_block, 0)

    def p_copy(d):
        other = lax.rem(me_d + d, n_dp)
        return remote(gp_send.at[other], gp_all.at[me_d], ps.at[d - 1], pr.at[me_d], dp=other)

    for d in range(1, n_dp):
        p_copy(d).start()
    gp_all[me_d] = gp_send[me_d]
    acc[...] = jnp.dot(table_t(me_z), back[me_z], preferred_element_type=F32)

    for d in range(1, n_dp):
        other = lax.rem(me_d + n_dp - d, n_dp)
        for block in range(n_exp):
            remote(
                x_all.at[other, block], x_all.at[other, block],
                fs.at[d - 1, block], fr.at[other, block], dp=other,
            ).wait_recv()
        remote(gp_send.at[other], gp_all.at[other], ps.at[d - 1], pr.at[other], dp=other).wait_recv()

    all_gp = gp_all[...].astype(F32).reshape(n_dp * n_exp * cap, part).astype(BF16)

    def out_copy(c):
        rows = pl.ds(pl.multiple_of(c * step, step), step)
        return pltpu.make_async_copy(gin_v.at[rows], gin_hbm.at[rows], outs.at[c])

    def one_chunk(c, carry):
        at = pl.ds(pl.multiple_of(c * step, step), step)
        xs_c = x_all[:, :, :, at].astype(F32).reshape(n_dp * n_exp * cap, step).astype(BF16)
        gin_v[at, :] = lax.dot_general(
            xs_c, all_gp, (((0,), (0,)), ((), ())), preferred_element_type=F32
        ).astype(BF16)
        out_copy(c).start()
        return carry

    lax.fori_loop(0, chunks, one_chunk, 0)

    for i in range(1, n_exp):
        block = from_of(i)
        remote(ret.at[i - 1], back.at[block], bs.at[i - 1], br.at[block], exp=block).wait_recv()
        total = acc[...] + jnp.dot(table_t(block), back[block], preferred_element_type=F32)
        if i < n_exp - 1:
            acc[...] = total
        else:
            gx_v[...] = total.astype(BF16)
    out_x = pltpu.make_async_copy(gx_v, gx_hbm, loc.at[3])
    out_x.start()

    seg_copy.wait_send()
    for i in range(1, n_exp):
        x_copy(i).wait_send()
        g_copy(i).wait_send()
        b_copy(i, from_of(i)).wait_send()
    for d in range(1, n_dp):
        for block in range(n_exp):
            forward(d, block).wait_send()
        p_copy(d).wait_send()
    for c in range(chunks):
        out_copy(c).wait()
    out_x.wait()


def hand_on(pieces, gx_ref, gin_ref, gx_out, gin_out, sems):
    copies = []
    for src, dst in ((gin_ref, gin_out), (gx_ref, gx_out)):
        rows = src.shape[0] // pieces
        for p in range(pieces):
            at = pl.ds(p * rows, rows)
            copies.append(pltpu.make_async_copy(src.at[at], dst.at[at], sems.at[len(copies)]))
    for copy in copies:
        copy.start()
    for copy in copies:
        copy.wait()


def body(saved_b, route_b, gate_b, grad_y_b, w_in, w_out):
    n_seg, n_dp, n_exp = lax.axis_size("segment"), lax.axis_size("dp"), lax.axis_size("expert")
    tok, width = saved_b.shape[1], saved_b.shape[2]
    hidden = w_in.shape[3]
    part = hidden // n_dp
    most = max(2, tok * 5 // (4 * n_exp))
    cap = -(-most // 8) * 8
    chunks = 4
    vmem = pl.BlockSpec(memory_space=pltpu.VMEM)
    hbm = pl.BlockSpec(memory_space=pl.ANY)
    dma = pltpu.SemaphoreType.DMA
    flops = 8 * n_exp * cap * width * hidden
    grad_x, grad_in = pl.pallas_call(
        functools.partial(kernel, (n_seg, n_dp, n_exp, cap, chunks)),
        out_shape=(
            jax.ShapeDtypeStruct((tok, width), BF16),
            jax.ShapeDtypeStruct((width, part), BF16),
        ),
        in_specs=[vmem, vmem, hbm, hbm, hbm, hbm],
        out_specs=(hbm, hbm),
        scratch_shapes=[
            pltpu.VMEM((tok, width), BF16),
            pltpu.VMEM((tok, width), BF16),
            pltpu.VMEM((width, hidden), BF16),
            pltpu.VMEM((hidden, width), BF16),
            pltpu.VMEM((n_exp - 1, cap, width), BF16),
            pltpu.VMEM((n_exp - 1, cap, width), BF16),
            pltpu.VMEM((n_dp, n_exp, cap, width), BF16),
            pltpu.VMEM((n_exp, cap, width), BF16),
            pltpu.VMEM((n_exp, cap, hidden), F32),
            pltpu.VMEM((n_dp, n_exp, cap, part), BF16),
            pltpu.VMEM((n_dp, n_exp, cap, part), BF16),
            pltpu.VMEM((n_exp - 1, cap, width), BF16),
            pltpu.VMEM((n_exp, cap, width), BF16),
            pltpu.VMEM((tok, width), F32),
            pltpu.VMEM((tok, width), BF16),
            pltpu.VMEM((width, part), BF16),
            dma((4,)),
            dma((1,)), dma((1,)),
            dma((n_exp,)), dma((n_exp,)),
            dma((n_exp,)), dma((n_exp,)),
            dma((n_dp, n_exp)), dma((n_dp, n_exp)),
            dma((n_dp,)), dma((n_dp,)),
            dma((n_exp,)), dma((n_exp,)),
            dma((chunks,)),
        ],
        compiler_params=pltpu.CompilerParams(
            collective_id=0, has_side_effects=True, vmem_limit_bytes=56 * 1024 * 1024
        ),
        cost_estimate=pl.CostEstimate(flops=flops, bytes_accessed=10 * 1024 * 1024, transcendentals=0),
    )(route_b.reshape(1, tok), gate_b.reshape(1, tok), saved_b, grad_y_b, w_in, w_out)
    pieces = 4
    grad_x, grad_in = pl.pallas_call(
        functools.partial(hand_on, pieces),
        out_shape=(
            jax.ShapeDtypeStruct((tok, width), BF16),
            jax.ShapeDtypeStruct((width, part), BF16),
        ),
        in_specs=[hbm, hbm],
        out_specs=(hbm, hbm),
        scratch_shapes=[dma((2 * pieces,))],
        compiler_params=pltpu.CompilerParams(vmem_limit_bytes=56 * 1024 * 1024),
    )(grad_x, grad_in)
    return (grad_x[None], grad_in[None, None])


def solution(mesh):
    return jax.shard_map(
        body,
        mesh=mesh,
        in_specs=(
            P("segment", ("dp", "expert"), None),
            P("segment", ("dp", "expert"), None),
            P("segment", ("dp", "expert"), None),
            P("segment", ("dp", "expert"), None),
            P("segment", "expert", None, None),
            P("segment", "expert", None, None),
        ),
        out_specs=(P("segment", ("dp", "expert"), None), P("segment", "expert", None, "dp")),
        check_vma=False,
    )
```

```python
import functools
import jax
import jax.numpy as jnp
from jax import lax
from jax.experimental import pallas as pl
from jax.experimental.pallas import tpu as pltpu
from jax.sharding import PartitionSpec as P

F32 = jnp.float32
BF16 = jnp.bfloat16


def kernel(
    sizes,
    route_ref, gate_ref, saved_hbm, gy_hbm, win_hbm, wout_hbm,
    gx_hbm, gin_hbm,
    saved_v, cot, win_v, wout_v, send_x, send_g, x_all, g_all, dsilu,
    gp_send, gp_all, ret, back, acc, gx_v, gin_v,
    loc, seg_s, seg_r, xs, xr, gs, gr, fs, fr, ps, pr, bs, br, outs,
):
    n_seg, n_dp, n_exp, cap, chunks = sizes
    me_s, me_d, me_z = lax.axis_index("segment"), lax.axis_index("dp"), lax.axis_index("expert")
    tok, width = saved_v.shape
    hidden = win_v.shape[1]
    part = hidden // n_dp
    step = width // chunks

    paired = n_exp & (n_exp - 1) == 0

    def flip(k):
        other, bit = me_z, 1
        while bit < n_exp:
            other = other + bit * (k // bit % 2) * (1 - 2 * (me_z // bit % 2))
            bit *= 2
        return other

    def to_of(k):
        return flip(k) if paired else lax.rem(me_z + k, n_exp)

    def from_of(k):
        return flip(k) if paired else lax.rem(me_z + n_exp - k, n_exp)

    half = max(1, n_exp // 2)
    inner = (me_z + half // 2) // half % 2

    def order(i, far_first):
        return 1 + lax.rem(i - 1 + far_first * (half - 1), max(1, n_exp - 1))

    def remote(src, dst, ss, rs, seg=None, dp=None, exp=None):
        dev = (
            me_s if seg is None else seg,
            me_d if dp is None else dp,
            me_z if exp is None else exp,
        )
        return pltpu.make_async_remote_copy(
            src_ref=src, dst_ref=dst, send_sem=ss, recv_sem=rs,
            device_id=dev, device_id_type=pl.DeviceIdType.MESH,
        )

    in_saved = pltpu.make_async_copy(saved_hbm.at[0], saved_v, loc.at[0])
    in_win = pltpu.make_async_copy(win_hbm.at[0, 0], win_v, loc.at[1])
    in_wout = pltpu.make_async_copy(wout_hbm.at[0, 0], wout_v, loc.at[2])
    in_saved.start()

    before_s = lax.rem(me_s + n_seg - 1, n_seg)
    after_s = lax.rem(me_s + 1, n_seg)
    barrier = pltpu.get_barrier_semaphore()
    peers = [(before_s, me_d, me_z), (after_s, me_d, me_z)]
    peers += [(me_s, lax.rem(me_d + d, n_dp), me_z) for d in range(1, n_dp)]
    peers += [(me_s, me_d, lax.rem(me_z + k, n_exp)) for k in range(1, n_exp)]
    for peer in peers:
        pl.semaphore_signal(barrier, inc=1, device_id=peer, device_id_type=pl.DeviceIdType.MESH)

    rows_t = lax.broadcasted_iota(jnp.int32, (tok, tok), 0)
    cols_t = lax.broadcasted_iota(jnp.int32, (tok, tok), 1)
    route = jnp.sum(jnp.where(rows_t == cols_t, route_ref[...], 0), axis=1, keepdims=True)
    gate = jnp.sum(jnp.where(rows_t == cols_t, gate_ref[...], 0.0), axis=1, keepdims=True)
    lanes = lax.broadcasted_iota(jnp.int32, (tok, 128), 1)
    onehot = (route == lanes).astype(F32)
    lower = (cols_t < rows_t).astype(BF16)
    ahead = jnp.dot(lower, onehot.astype(BF16), preferred_element_type=F32)
    rank = jnp.sum(ahead * onehot, axis=1, keepdims=True).astype(jnp.int32)
    pos_col = route * cap + rank
    pos_row = jnp.sum(jnp.where(rows_t == cols_t, pos_col, 0), axis=0, keepdims=True)

    def table(expert):
        slots = lax.broadcasted_iota(jnp.int32, (cap, tok), 0) + expert * cap
        return (slots == pos_row).astype(F32).astype(BF16)

    def table_t(expert):
        slots = lax.broadcasted_iota(jnp.int32, (tok, cap), 1) + expert * cap
        return (slots == pos_col).astype(F32).astype(BF16)

    pl.semaphore_wait(barrier, len(peers))
    seg_copy = remote(gy_hbm.at[0], cot, seg_s.at[0], seg_r.at[0], seg=before_s)
    seg_copy.start()
    in_saved.wait()
    saved = saved_v[...]

    def x_copy(i):
        return remote(send_x.at[i - 1], x_all.at[me_d, me_z], xs.at[i - 1], xr.at[me_z], exp=to_of(i))

    for i in range(1, n_exp):
        k = order(i, inner)
        send_x[k - 1] = jnp.dot(table(to_of(k)), saved, preferred_element_type=F32).astype(BF16)
        x_copy(k).start()
    in_win.start()
    in_wout.start()
    x_all[me_d, me_z] = jnp.dot(table(me_z), saved, preferred_element_type=F32).astype(BF16)

    def forward(d, block):
        return remote(
            x_all.at[me_d, block], x_all.at[me_d, block],
            fs.at[d - 1, block], fr.at[me_d, block], dp=lax.rem(me_d + d, n_dp),
        )

    for d in range(1, n_dp):
        forward(d, me_z).start()

    seg_copy.wait_recv()
    scaled = (gate * cot[...].astype(F32)).astype(BF16)

    def g_copy(i):
        return remote(send_g.at[i - 1], g_all.at[me_z], gs.at[i - 1], gr.at[me_z], exp=to_of(i))

    for i in range(1, n_exp):
        k = order(i, inner)
        send_g[k - 1] = jnp.dot(table(to_of(k)), scaled, preferred_element_type=F32).astype(BF16)
        g_copy(k).start()
    g_all[me_z] = jnp.dot(table(me_z), scaled, preferred_element_type=F32).astype(BF16)

    for i in range(1, n_exp):
        k = order(i, 1 - inner)
        block = from_of(k)
        remote(send_x.at[k - 1], x_all.at[me_d, block], xs.at[k - 1], xr.at[block], exp=block).wait_recv()
        for d in range(1, n_dp):
            forward(d, block).start()

    in_win.wait()
    own_x = x_all[me_d].astype(F32).reshape(n_exp * cap, width).astype(BF16)
    pre = jnp.dot(own_x, win_v[...], preferred_element_type=F32)
    sigma = jax.nn.sigmoid(pre)
    dsilu[...] = (sigma * (1.0 + pre * (1.0 - sigma))).reshape(n_exp, cap, hidden)
    in_wout.wait()

    def expert_block(block):
        grad_h = lax.dot_general(
            g_all[block], wout_v[...], (((1,), (1,)), ((), ())), preferred_element_type=F32
        )
        grad_pre = (grad_h * dsilu[block]).astype(BF16)
        for j in range(n_dp):
            gp_send[j, block] = grad_pre[:, j * part:(j + 1) * part]
        return lax.dot_general(
            grad_pre, win_v[...], (((1,), (1,)), ((), ())), preferred_element_type=F32
        ).astype(BF16)

    def b_copy(i, block):
        return remote(ret.at[i - 1], back.at[me_z], bs.at[i - 1], br.at[me_z], exp=block)

    back[me_z] = expert_block(me_z)

    def one_block(i, carry):
        k = order(i, 1 - inner)
        block = from_of(k)
        remote(send_g.at[k - 1], g_all.at[block], gs.at[k - 1], gr.at[block], exp=block).wait_recv()
        ret[k - 1] = expert_block(block)
        b_copy(k, block).start()
        return carry

    lax.fori_loop(1, n_exp, one_block, 0)

    def p_copy(d):
        other = lax.rem(me_d + d, n_dp)
        return remote(gp_send.at[other], gp_all.at[me_d], ps.at[d - 1], pr.at[me_d], dp=other)

    for d in range(1, n_dp):
        p_copy(d).start()
    gp_all[me_d] = gp_send[me_d]
    acc[...] = jnp.dot(table_t(me_z), back[me_z], preferred_element_type=F32)

    for d in range(1, n_dp):
        other = lax.rem(me_d + n_dp - d, n_dp)
        for block in range(n_exp):
            remote(
                x_all.at[other, block], x_all.at[other, block],
                fs.at[d - 1, block], fr.at[other, block], dp=other,
            ).wait_recv()
        remote(gp_send.at[other], gp_all.at[other], ps.at[d - 1], pr.at[other], dp=other).wait_recv()

    all_gp = gp_all[...].astype(F32).reshape(n_dp * n_exp * cap, part).astype(BF16)

    def out_copy(c):
        rows = pl.ds(pl.multiple_of(c * step, step), step)
        return pltpu.make_async_copy(gin_v.at[rows], gin_hbm.at[rows], outs.at[c])

    def one_chunk(c, carry):
        at = pl.ds(pl.multiple_of(c * step, step), step)
        xs_c = x_all[:, :, :, at].astype(F32).reshape(n_dp * n_exp * cap, step).astype(BF16)
        gin_v[at, :] = lax.dot_general(
            xs_c, all_gp, (((0,), (0,)), ((), ())), preferred_element_type=F32
        ).astype(BF16)
        out_copy(c).start()
        return carry

    lax.fori_loop(0, chunks, one_chunk, 0)

    for i in range(1, n_exp):
        k = order(i, inner)
        block = to_of(k)
        remote(ret.at[k - 1], back.at[block], bs.at[k - 1], br.at[block], exp=block).wait_recv()
        total = acc[...] + jnp.dot(table_t(block), back[block], preferred_element_type=F32)
        if i < n_exp - 1:
            acc[...] = total
        else:
            gx_v[...] = total.astype(BF16)
    out_x = pltpu.make_async_copy(gx_v, gx_hbm, loc.at[3])
    out_x.start()

    seg_copy.wait_send()
    for i in range(1, n_exp):
        x_copy(i).wait_send()
        g_copy(i).wait_send()
        b_copy(i, from_of(i)).wait_send()
    for d in range(1, n_dp):
        for block in range(n_exp):
            forward(d, block).wait_send()
        p_copy(d).wait_send()
    for c in range(chunks):
        out_copy(c).wait()
    out_x.wait()


def hand_on(pieces, gx_ref, gin_ref, gx_out, gin_out, gx_v, gin_v, sems):
    loads, stores = [], []
    for src, mid, dst in ((gin_ref, gin_v, gin_out), (gx_ref, gx_v, gx_out)):
        rows = src.shape[0] // pieces
        for p in range(pieces):
            at = pl.ds(p * rows, rows)
            loads.append(pltpu.make_async_copy(src.at[at], mid.at[at], sems.at[0, len(loads)]))
            stores.append(pltpu.make_async_copy(mid.at[at], dst.at[at], sems.at[1, len(stores)]))
    for load in loads:
        load.start()
    for load, store in zip(loads, stores):
        load.wait()
        store.start()
    for store in stores:
        store.wait()


def body(saved_b, route_b, gate_b, grad_y_b, w_in, w_out):
    n_seg, n_dp, n_exp = lax.axis_size("segment"), lax.axis_size("dp"), lax.axis_size("expert")
    tok, width = saved_b.shape[1], saved_b.shape[2]
    hidden = w_in.shape[3]
    part = hidden // n_dp
    most = max(2, tok * 5 // (4 * n_exp))
    cap = -(-most // 8) * 8
    chunks = 4
    vmem = pl.BlockSpec(memory_space=pltpu.VMEM)
    hbm = pl.BlockSpec(memory_space=pl.ANY)
    dma = pltpu.SemaphoreType.DMA
    flops = 8 * n_exp * cap * width * hidden
    grad_x, grad_in = pl.pallas_call(
        functools.partial(kernel, (n_seg, n_dp, n_exp, cap, chunks)),
        out_shape=(
            jax.ShapeDtypeStruct((tok, width), BF16),
            jax.ShapeDtypeStruct((width, part), BF16),
        ),
        in_specs=[vmem, vmem, hbm, hbm, hbm, hbm],
        out_specs=(hbm, hbm),
        scratch_shapes=[
            pltpu.VMEM((tok, width), BF16),
            pltpu.VMEM((tok, width), BF16),
            pltpu.VMEM((width, hidden), BF16),
            pltpu.VMEM((hidden, width), BF16),
            pltpu.VMEM((n_exp - 1, cap, width), BF16),
            pltpu.VMEM((n_exp - 1, cap, width), BF16),
            pltpu.VMEM((n_dp, n_exp, cap, width), BF16),
            pltpu.VMEM((n_exp, cap, width), BF16),
            pltpu.VMEM((n_exp, cap, hidden), F32),
            pltpu.VMEM((n_dp, n_exp, cap, part), BF16),
            pltpu.VMEM((n_dp, n_exp, cap, part), BF16),
            pltpu.VMEM((n_exp - 1, cap, width), BF16),
            pltpu.VMEM((n_exp, cap, width), BF16),
            pltpu.VMEM((tok, width), F32),
            pltpu.VMEM((tok, width), BF16),
            pltpu.VMEM((width, part), BF16),
            dma((4,)),
            dma((1,)), dma((1,)),
            dma((n_exp,)), dma((n_exp,)),
            dma((n_exp,)), dma((n_exp,)),
            dma((n_dp, n_exp)), dma((n_dp, n_exp)),
            dma((n_dp,)), dma((n_dp,)),
            dma((n_exp,)), dma((n_exp,)),
            dma((chunks,)),
        ],
        compiler_params=pltpu.CompilerParams(
            collective_id=0, has_side_effects=True, vmem_limit_bytes=56 * 1024 * 1024
        ),
        cost_estimate=pl.CostEstimate(flops=flops, bytes_accessed=10 * 1024 * 1024, transcendentals=0),
    )(route_b.reshape(1, tok), gate_b.reshape(1, tok), saved_b, grad_y_b, w_in, w_out)
    pieces = 4
    grad_x, grad_in = pl.pallas_call(
        functools.partial(hand_on, pieces),
        out_shape=(
            jax.ShapeDtypeStruct((tok, width), BF16),
            jax.ShapeDtypeStruct((width, part), BF16),
        ),
        in_specs=[hbm, hbm],
        out_specs=(hbm, hbm),
        scratch_shapes=[
            pltpu.VMEM((tok, width), BF16), pltpu.VMEM((width, part), BF16), dma((2, 2 * pieces)),
        ],
        compiler_params=pltpu.CompilerParams(vmem_limit_bytes=56 * 1024 * 1024),
    )(grad_x, grad_in)
    return (grad_x[None], grad_in[None, None])


def solution(mesh):
    return jax.shard_map(
        body,
        mesh=mesh,
        in_specs=(
            P("segment", ("dp", "expert"), None),
            P("segment", ("dp", "expert"), None),
            P("segment", ("dp", "expert"), None),
            P("segment", ("dp", "expert"), None),
            P("segment", "expert", None, None),
            P("segment", "expert", None, None),
        ),
        out_specs=(P("segment", ("dp", "expert"), None), P("segment", "expert", None, "dp")),
        check_vma=False,
    )
```

```python
import functools
import jax
import jax.numpy as jnp
from jax import lax
from jax.experimental import pallas as pl
from jax.experimental.pallas import tpu as pltpu
from jax.sharding import PartitionSpec as P

F32 = jnp.float32
BF16 = jnp.bfloat16


def kernel(
    sizes,
    route_ref, gate_ref, saved_hbm, gy_hbm, win_hbm, wout_hbm,
    gx_hbm, gin_hbm,
    saved_v, cot, win_v, wout_v, send_x, send_g, x_all, g_all, dsilu,
    gp_send, gp_all, ret, back, acc, gx_v, gin_v,
    loc, seg_s, seg_r, xs, xr, gs, gr, fs, fr, ps, pr, bs, br, outs,
):
    n_seg, n_dp, n_exp, cap, chunks = sizes
    me_s, me_d, me_z = lax.axis_index("segment"), lax.axis_index("dp"), lax.axis_index("expert")
    tok, width = saved_v.shape
    hidden = win_v.shape[1]
    part = hidden // n_dp
    step = width // chunks

    paired = n_exp & (n_exp - 1) == 0

    def flip(k):
        other, bit = me_z, 1
        while bit < n_exp:
            other = other + bit * (k // bit % 2) * (1 - 2 * (me_z // bit % 2))
            bit *= 2
        return other

    def to_of(k):
        return flip(k) if paired else lax.rem(me_z + k, n_exp)

    def from_of(k):
        return flip(k) if paired else lax.rem(me_z + n_exp - k, n_exp)

    half = max(1, n_exp // 2)
    inner = (me_z + half // 2) // half % 2

    def order(i, far_first):
        return 1 + lax.rem(i - 1 + far_first * (half - 1), max(1, n_exp - 1))

    def remote(src, dst, ss, rs, seg=None, dp=None, exp=None):
        dev = (
            me_s if seg is None else seg,
            me_d if dp is None else dp,
            me_z if exp is None else exp,
        )
        return pltpu.make_async_remote_copy(
            src_ref=src, dst_ref=dst, send_sem=ss, recv_sem=rs,
            device_id=dev, device_id_type=pl.DeviceIdType.MESH,
        )

    in_saved = pltpu.make_async_copy(saved_hbm.at[0], saved_v, loc.at[0])
    in_win = pltpu.make_async_copy(win_hbm.at[0, 0], win_v, loc.at[1])
    in_wout = pltpu.make_async_copy(wout_hbm.at[0, 0], wout_v, loc.at[2])
    in_saved.start()

    before_s = lax.rem(me_s + n_seg - 1, n_seg)
    after_s = lax.rem(me_s + 1, n_seg)
    barrier = pltpu.get_barrier_semaphore()
    peers = [(before_s, me_d, me_z), (after_s, me_d, me_z)]
    peers += [(me_s, lax.rem(me_d + d, n_dp), me_z) for d in range(1, n_dp)]
    peers += [(me_s, me_d, lax.rem(me_z + k, n_exp)) for k in range(1, n_exp)]
    for peer in peers:
        pl.semaphore_signal(barrier, inc=1, device_id=peer, device_id_type=pl.DeviceIdType.MESH)

    rows_t = lax.broadcasted_iota(jnp.int32, (tok, tok), 0)
    cols_t = lax.broadcasted_iota(jnp.int32, (tok, tok), 1)
    route = jnp.sum(jnp.where(rows_t == cols_t, route_ref[...], 0), axis=1, keepdims=True)
    gate = jnp.sum(jnp.where(rows_t == cols_t, gate_ref[...], 0.0), axis=1, keepdims=True)
    lanes = lax.broadcasted_iota(jnp.int32, (tok, 128), 1)
    onehot = (route == lanes).astype(F32)
    lower = (cols_t < rows_t).astype(BF16)
    ahead = jnp.dot(lower, onehot.astype(BF16), preferred_element_type=F32)
    rank = jnp.sum(ahead * onehot, axis=1, keepdims=True).astype(jnp.int32)
    pos_col = route * cap + rank
    pos_row = jnp.sum(jnp.where(rows_t == cols_t, pos_col, 0), axis=0, keepdims=True)

    def table(expert):
        slots = lax.broadcasted_iota(jnp.int32, (cap, tok), 0) + expert * cap
        return (slots == pos_row).astype(F32).astype(BF16)

    def table_t(expert):
        slots = lax.broadcasted_iota(jnp.int32, (tok, cap), 1) + expert * cap
        return (slots == pos_col).astype(F32).astype(BF16)

    pl.semaphore_wait(barrier, len(peers))
    seg_copy = remote(gy_hbm.at[0], cot, seg_s.at[0], seg_r.at[0], seg=before_s)
    seg_copy.start()
    in_saved.wait()
    saved = saved_v[...]

    def x_copy(i):
        return remote(send_x.at[i - 1], x_all.at[me_d, i], xs.at[i - 1], xr.at[i], exp=to_of(i))

    for i in range(1, n_exp):
        k = order(i, inner)
        send_x[k - 1] = jnp.dot(table(to_of(k)), saved, preferred_element_type=F32).astype(BF16)
        x_copy(k).start()
    in_win.start()
    in_wout.start()
    x_all[me_d, 0] = jnp.dot(table(me_z), saved, preferred_element_type=F32).astype(BF16)

    def forward(d, block):
        return remote(
            x_all.at[me_d, block], x_all.at[me_d, block],
            fs.at[d - 1, block], fr.at[me_d, block], dp=lax.rem(me_d + d, n_dp),
        )

    for d in range(1, n_dp):
        forward(d, 0).start()

    seg_copy.wait_recv()
    scaled = (gate * cot[...].astype(F32)).astype(BF16)

    def g_copy(i):
        return remote(send_g.at[i - 1], g_all.at[i], gs.at[i - 1], gr.at[i], exp=to_of(i))

    for i in range(1, n_exp):
        k = order(i, inner)
        send_g[k - 1] = jnp.dot(table(to_of(k)), scaled, preferred_element_type=F32).astype(BF16)
        g_copy(k).start()
    g_all[0] = jnp.dot(table(me_z), scaled, preferred_element_type=F32).astype(BF16)

    for i in range(1, n_exp):
        k = order(i, 1 - inner)
        remote(send_x.at[k - 1], x_all.at[me_d, k], xs.at[k - 1], xr.at[k], exp=from_of(k)).wait_recv()
        for d in range(1, n_dp):
            forward(d, k).start()

    in_win.wait()
    own_x = x_all[me_d].astype(F32).reshape(n_exp * cap, width).astype(BF16)
    pre = jnp.dot(own_x, win_v[...], preferred_element_type=F32)
    sigma = jax.nn.sigmoid(pre)
    dsilu[...] = (sigma * (1.0 + pre * (1.0 - sigma))).reshape(n_exp, cap, hidden)
    in_wout.wait()

    def g_wait(k):
        remote(send_g.at[k - 1], g_all.at[k], gs.at[k - 1], gr.at[k], exp=from_of(k)).wait_recv()

    def b_copy(k):
        return remote(ret.at[k - 1], back.at[k], bs.at[k - 1], br.at[k], exp=from_of(k))

    def expert_blocks(first, last):
        count = last - first
        rows = g_all[first:last].astype(F32).reshape(count * cap, width).astype(BF16)
        grad_h = lax.dot_general(
            rows, wout_v[...], (((1,), (1,)), ((), ())), preferred_element_type=F32
        )
        scale = dsilu[first:last].reshape(count * cap, hidden)
        grad_pre = (grad_h * scale).astype(BF16)
        grad_x = lax.dot_general(
            grad_pre, win_v[...], (((1,), (1,)), ((), ())), preferred_element_type=F32
        ).reshape(count, cap, width)
        for k in range(first, last):
            if k:
                ret[k - 1] = grad_x[k - first].astype(BF16)
                b_copy(k).start()
            else:
                back[0] = grad_x[0].astype(BF16)
        wide = grad_pre.astype(F32).reshape(count, cap, hidden).astype(BF16)
        for j in range(n_dp):
            gp_send[j, first:last] = wide[:, :, j * part:(j + 1) * part]

    for k in range(1, half):
        g_wait(k)
    expert_blocks(0, half)
    for k in range(half, n_exp):
        g_wait(k)
    expert_blocks(half, n_exp)

    def p_copy(d):
        other = lax.rem(me_d + d, n_dp)
        return remote(gp_send.at[other], gp_all.at[me_d], ps.at[d - 1], pr.at[me_d], dp=other)

    for d in range(1, n_dp):
        p_copy(d).start()
    gp_all[me_d] = gp_send[me_d]
    acc[...] = jnp.dot(table_t(me_z), back[0], preferred_element_type=F32)

    for d in range(1, n_dp):
        other = lax.rem(me_d + n_dp - d, n_dp)
        for block in range(n_exp):
            remote(
                x_all.at[other, block], x_all.at[other, block],
                fs.at[d - 1, block], fr.at[other, block], dp=other,
            ).wait_recv()
        remote(gp_send.at[other], gp_all.at[other], ps.at[d - 1], pr.at[other], dp=other).wait_recv()

    all_gp = gp_all[...].astype(F32).reshape(n_dp * n_exp * cap, part).astype(BF16)

    def out_copy(c):
        rows = pl.ds(pl.multiple_of(c * step, step), step)
        return pltpu.make_async_copy(gin_v.at[rows], gin_hbm.at[rows], outs.at[c])

    def one_chunk(c, carry):
        at = pl.ds(pl.multiple_of(c * step, step), step)
        xs_c = x_all[:, :, :, at].astype(F32).reshape(n_dp * n_exp * cap, step).astype(BF16)
        gin_v[at, :] = lax.dot_general(
            xs_c, all_gp, (((0,), (0,)), ((), ())), preferred_element_type=F32
        ).astype(BF16)
        out_copy(c).start()
        return carry

    lax.fori_loop(0, chunks, one_chunk, 0)

    for i in range(1, n_exp):
        k = order(i, inner)
        remote(ret.at[k - 1], back.at[k], bs.at[k - 1], br.at[k], exp=to_of(k)).wait_recv()
        total = acc[...] + jnp.dot(table_t(to_of(k)), back[k], preferred_element_type=F32)
        if i < n_exp - 1:
            acc[...] = total
        else:
            gx_v[...] = total.astype(BF16)
    out_x = pltpu.make_async_copy(gx_v, gx_hbm, loc.at[3])
    out_x.start()

    seg_copy.wait_send()
    for i in range(1, n_exp):
        x_copy(i).wait_send()
        g_copy(i).wait_send()
        b_copy(i).wait_send()
    for d in range(1, n_dp):
        for block in range(n_exp):
            forward(d, block).wait_send()
        p_copy(d).wait_send()
    for c in range(chunks):
        out_copy(c).wait()
    out_x.wait()


def hand_on(pieces, gx_ref, gin_ref, gx_out, gin_out, gx_v, gin_v, sems):
    loads, stores = [], []
    for src, mid, dst in ((gin_ref, gin_v, gin_out), (gx_ref, gx_v, gx_out)):
        rows = src.shape[0] // pieces
        for p in range(pieces):
            at = pl.ds(p * rows, rows)
            loads.append(pltpu.make_async_copy(src.at[at], mid.at[at], sems.at[0, len(loads)]))
            stores.append(pltpu.make_async_copy(mid.at[at], dst.at[at], sems.at[1, len(stores)]))
    for load in loads:
        load.start()
    for load, store in zip(loads, stores):
        load.wait()
        store.start()
    for store in stores:
        store.wait()


def body(saved_b, route_b, gate_b, grad_y_b, w_in, w_out):
    n_seg, n_dp, n_exp = lax.axis_size("segment"), lax.axis_size("dp"), lax.axis_size("expert")
    tok, width = saved_b.shape[1], saved_b.shape[2]
    hidden = w_in.shape[3]
    part = hidden // n_dp
    most = max(2, tok * 5 // (4 * n_exp))
    cap = -(-most // 8) * 8
    chunks = 4
    vmem = pl.BlockSpec(memory_space=pltpu.VMEM)
    hbm = pl.BlockSpec(memory_space=pl.ANY)
    dma = pltpu.SemaphoreType.DMA
    flops = 8 * n_exp * cap * width * hidden
    grad_x, grad_in = pl.pallas_call(
        functools.partial(kernel, (n_seg, n_dp, n_exp, cap, chunks)),
        out_shape=(
            jax.ShapeDtypeStruct((tok, width), BF16),
            jax.ShapeDtypeStruct((width, part), BF16),
        ),
        in_specs=[vmem, vmem, hbm, hbm, hbm, hbm],
        out_specs=(hbm, hbm),
        scratch_shapes=[
            pltpu.VMEM((tok, width), BF16),
            pltpu.VMEM((tok, width), BF16),
            pltpu.VMEM((width, hidden), BF16),
            pltpu.VMEM((hidden, width), BF16),
            pltpu.VMEM((n_exp - 1, cap, width), BF16),
            pltpu.VMEM((n_exp - 1, cap, width), BF16),
            pltpu.VMEM((n_dp, n_exp, cap, width), BF16),
            pltpu.VMEM((n_exp, cap, width), BF16),
            pltpu.VMEM((n_exp, cap, hidden), F32),
            pltpu.VMEM((n_dp, n_exp, cap, part), BF16),
            pltpu.VMEM((n_dp, n_exp, cap, part), BF16),
            pltpu.VMEM((n_exp - 1, cap, width), BF16),
            pltpu.VMEM((n_exp, cap, width), BF16),
            pltpu.VMEM((tok, width), F32),
            pltpu.VMEM((tok, width), BF16),
            pltpu.VMEM((width, part), BF16),
            dma((4,)),
            dma((1,)), dma((1,)),
            dma((n_exp,)), dma((n_exp,)),
            dma((n_exp,)), dma((n_exp,)),
            dma((n_dp, n_exp)), dma((n_dp, n_exp)),
            dma((n_dp,)), dma((n_dp,)),
            dma((n_exp,)), dma((n_exp,)),
            dma((chunks,)),
        ],
        compiler_params=pltpu.CompilerParams(
            collective_id=0, has_side_effects=True, vmem_limit_bytes=56 * 1024 * 1024
        ),
        cost_estimate=pl.CostEstimate(flops=flops, bytes_accessed=10 * 1024 * 1024, transcendentals=0),
    )(route_b.reshape(1, tok), gate_b.reshape(1, tok), saved_b, grad_y_b, w_in, w_out)
    pieces = 4
    grad_x, grad_in = pl.pallas_call(
        functools.partial(hand_on, pieces),
        out_shape=(
            jax.ShapeDtypeStruct((tok, width), BF16),
            jax.ShapeDtypeStruct((width, part), BF16),
        ),
        in_specs=[hbm, hbm],
        out_specs=(hbm, hbm),
        scratch_shapes=[
            pltpu.VMEM((tok, width), BF16), pltpu.VMEM((width, part), BF16), dma((2, 2 * pieces)),
        ],
        compiler_params=pltpu.CompilerParams(vmem_limit_bytes=56 * 1024 * 1024),
    )(grad_x, grad_in)
    return (grad_x[None], grad_in[None, None])


def solution(mesh):
    return jax.shard_map(
        body,
        mesh=mesh,
        in_specs=(
            P("segment", ("dp", "expert"), None),
            P("segment", ("dp", "expert"), None),
            P("segment", ("dp", "expert"), None),
            P("segment", ("dp", "expert"), None),
            P("segment", "expert", None, None),
            P("segment", "expert", None, None),
        ),
        out_specs=(P("segment", ("dp", "expert"), None), P("segment", "expert", None, "dp")),
        check_vma=False,
    )
```

```python
import functools
import jax
import jax.numpy as jnp
from jax import lax
from jax.experimental import pallas as pl
from jax.experimental.pallas import tpu as pltpu
from jax.sharding import PartitionSpec as P

F32 = jnp.float32
BF16 = jnp.bfloat16


def kernel(
    sizes,
    route_ref, gate_ref, saved_hbm, gy_hbm, win_hbm, wout_hbm,
    back, pick_hbm, gin_hbm,
    saved_v, cot, win_v, wout_v, send_x, send_g, x_all, g_all, dsilu,
    gp_send, gp_all, ret, own_ret, pick, gin_v,
    loc, seg_s, seg_r, xs, xr, gs, gr, fs, fr, ps, pr, bs, br, outs,
):
    n_seg, n_dp, n_exp, cap, chunks = sizes
    me_s, me_d, me_z = lax.axis_index("segment"), lax.axis_index("dp"), lax.axis_index("expert")
    tok, width = saved_v.shape
    hidden = win_v.shape[1]
    part = hidden // n_dp
    step = width // chunks

    paired = n_exp & (n_exp - 1) == 0

    def flip(k):
        other, bit = me_z, 1
        while bit < n_exp:
            other = other + bit * (k // bit % 2) * (1 - 2 * (me_z // bit % 2))
            bit *= 2
        return other

    def to_of(k):
        return flip(k) if paired else lax.rem(me_z + k, n_exp)

    def from_of(k):
        return flip(k) if paired else lax.rem(me_z + n_exp - k, n_exp)

    half = max(1, n_exp // 2)
    inner = (me_z + half // 2) // half % 2

    def order(i, far_first):
        return 1 + lax.rem(i - 1 + far_first * (half - 1), max(1, n_exp - 1))

    def remote(src, dst, ss, rs, seg=None, dp=None, exp=None):
        dev = (
            me_s if seg is None else seg,
            me_d if dp is None else dp,
            me_z if exp is None else exp,
        )
        return pltpu.make_async_remote_copy(
            src_ref=src, dst_ref=dst, send_sem=ss, recv_sem=rs,
            device_id=dev, device_id_type=pl.DeviceIdType.MESH,
        )

    in_saved = pltpu.make_async_copy(saved_hbm.at[0], saved_v, loc.at[0])
    in_win = pltpu.make_async_copy(win_hbm.at[0, 0], win_v, loc.at[1])
    in_wout = pltpu.make_async_copy(wout_hbm.at[0, 0], wout_v, loc.at[2])
    in_saved.start()

    before_s = lax.rem(me_s + n_seg - 1, n_seg)
    after_s = lax.rem(me_s + 1, n_seg)
    barrier = pltpu.get_barrier_semaphore()
    peers = [(before_s, me_d, me_z), (after_s, me_d, me_z)]
    peers += [(me_s, lax.rem(me_d + d, n_dp), me_z) for d in range(1, n_dp)]
    peers += [(me_s, me_d, lax.rem(me_z + k, n_exp)) for k in range(1, n_exp)]
    for peer in peers:
        pl.semaphore_signal(barrier, inc=1, device_id=peer, device_id_type=pl.DeviceIdType.MESH)

    rows_t = lax.broadcasted_iota(jnp.int32, (tok, tok), 0)
    cols_t = lax.broadcasted_iota(jnp.int32, (tok, tok), 1)
    route = jnp.sum(jnp.where(rows_t == cols_t, route_ref[...], 0), axis=1, keepdims=True)
    gate = jnp.sum(jnp.where(rows_t == cols_t, gate_ref[...], 0.0), axis=1, keepdims=True)
    lanes = lax.broadcasted_iota(jnp.int32, (tok, 128), 1)
    onehot = (route == lanes).astype(F32)
    lower = (cols_t < rows_t).astype(BF16)
    ahead = jnp.dot(lower, onehot.astype(BF16), preferred_element_type=F32)
    rank = jnp.sum(ahead * onehot, axis=1, keepdims=True).astype(jnp.int32)
    pos_col = route * cap + rank
    pos_row = jnp.sum(jnp.where(rows_t == cols_t, pos_col, 0), axis=0, keepdims=True)

    def table(expert):
        slots = lax.broadcasted_iota(jnp.int32, (cap, tok), 0) + expert * cap
        return (slots == pos_row).astype(F32).astype(BF16)

    if paired:
        apart, bit = route * 0, 1
        while bit < n_exp:
            one, two = route // bit % 2, me_z // bit % 2
            apart = apart + bit * (one + two - 2 * one * two)
            bit *= 2
    else:
        apart = lax.rem(route + n_exp - me_z, n_exp)
    places = lax.broadcasted_iota(jnp.int32, (tok, n_exp * cap), 1)
    pick[...] = (places == apart * cap + rank).astype(F32).astype(BF16)
    out_pick = pltpu.make_async_copy(pick, pick_hbm, loc.at[4])
    out_pick.start()

    in_saved.wait()
    saved = saved_v[...]
    for i in range(1, n_exp):
        send_x[i - 1] = jnp.dot(table(to_of(i)), saved, preferred_element_type=F32).astype(BF16)

    pl.semaphore_wait(barrier, len(peers))
    seg_copy = remote(gy_hbm.at[0], cot, seg_s.at[0], seg_r.at[0], seg=before_s)
    seg_copy.start()

    def x_copy(i):
        return remote(send_x.at[i - 1], x_all.at[me_d, i], xs.at[i - 1], xr.at[i], exp=to_of(i))

    for i in range(1, n_exp):
        x_copy(order(i, inner)).start()
    in_win.start()
    in_wout.start()
    x_all[me_d, 0] = jnp.dot(table(me_z), saved, preferred_element_type=F32).astype(BF16)

    def forward(d, block):
        return remote(
            x_all.at[me_d, block], x_all.at[me_d, block],
            fs.at[d - 1, block], fr.at[me_d, block], dp=lax.rem(me_d + d, n_dp),
        )

    for d in range(1, n_dp):
        forward(d, 0).start()

    seg_copy.wait_recv()
    scaled = (gate * cot[...].astype(F32)).astype(BF16)

    def g_copy(i):
        return remote(send_g.at[i - 1], g_all.at[i], gs.at[i - 1], gr.at[i], exp=to_of(i))

    for i in range(1, n_exp):
        send_g[i - 1] = jnp.dot(table(to_of(i)), scaled, preferred_element_type=F32).astype(BF16)
        g_copy(i).start()
    g_all[0] = jnp.dot(table(me_z), scaled, preferred_element_type=F32).astype(BF16)

    for i in range(1, n_exp):
        k = order(i, 1 - inner)
        remote(send_x.at[k - 1], x_all.at[me_d, k], xs.at[k - 1], xr.at[k], exp=from_of(k)).wait_recv()
        for d in range(1, n_dp):
            forward(d, k).start()

    in_win.wait()
    own_x = x_all[me_d].astype(F32).reshape(n_exp * cap, width).astype(BF16)
    pre = jnp.dot(own_x, win_v[...], preferred_element_type=F32)
    sigma = jax.nn.sigmoid(pre)
    dsilu[...] = (sigma * (1.0 + pre * (1.0 - sigma))).reshape(n_exp, cap, hidden)
    in_wout.wait()

    def g_wait(k):
        remote(send_g.at[k - 1], g_all.at[k], gs.at[k - 1], gr.at[k], exp=from_of(k)).wait_recv()

    def b_copy(k):
        return remote(ret.at[k - 1], back.at[k], bs.at[k - 1], br.at[k], exp=from_of(k))

    own_back = pltpu.make_async_copy(own_ret, back.at[0], loc.at[3])

    def expert_blocks(first, last):
        count = last - first
        rows = g_all[first:last].astype(F32).reshape(count * cap, width).astype(BF16)
        grad_h = lax.dot_general(
            rows, wout_v[...], (((1,), (1,)), ((), ())), preferred_element_type=F32
        )
        scale = dsilu[first:last].reshape(count * cap, hidden)
        grad_pre = (grad_h * scale).astype(BF16)
        grad_x = lax.dot_general(
            grad_pre, win_v[...], (((1,), (1,)), ((), ())), preferred_element_type=F32
        ).reshape(count, cap, width)
        for k in range(first, last):
            if k:
                ret[k - 1] = grad_x[k - first].astype(BF16)
                b_copy(k).start()
            else:
                own_ret[...] = grad_x[0].astype(BF16)
                own_back.start()
        wide = grad_pre.astype(F32).reshape(count, cap, hidden).astype(BF16)
        for j in range(n_dp):
            gp_send[j, first:last] = wide[:, :, j * part:(j + 1) * part]

    for k in range(1, half):
        g_wait(k)
    expert_blocks(0, half)
    for k in range(half, n_exp):
        g_wait(k)
        expert_blocks(k, k + 1)

    def p_copy(d):
        other = lax.rem(me_d + d, n_dp)
        return remote(gp_send.at[other], gp_all.at[me_d], ps.at[d - 1], pr.at[me_d], dp=other)

    for d in range(1, n_dp):
        p_copy(d).start()
    gp_all[me_d] = gp_send[me_d]

    for d in range(1, n_dp):
        other = lax.rem(me_d + n_dp - d, n_dp)
        for block in range(n_exp):
            remote(
                x_all.at[other, block], x_all.at[other, block],
                fs.at[d - 1, block], fr.at[other, block], dp=other,
            ).wait_recv()
        remote(gp_send.at[other], gp_all.at[other], ps.at[d - 1], pr.at[other], dp=other).wait_recv()

    all_gp = gp_all[...].astype(F32).reshape(n_dp * n_exp * cap, part).astype(BF16)

    def out_copy(c):
        rows = pl.ds(pl.multiple_of(c * step, step), step)
        return pltpu.make_async_copy(gin_v.at[rows], gin_hbm.at[rows], outs.at[c])

    def one_chunk(c, carry):
        at = pl.ds(pl.multiple_of(c * step, step), step)
        xs_c = x_all[:, :, :, at].astype(F32).reshape(n_dp * n_exp * cap, step).astype(BF16)
        gin_v[at, :] = lax.dot_general(
            xs_c, all_gp, (((0,), (0,)), ((), ())), preferred_element_type=F32
        ).astype(BF16)
        out_copy(c).start()
        return carry

    lax.fori_loop(0, chunks, one_chunk, 0)

    for k in range(1, n_exp):
        remote(ret.at[k - 1], back.at[k], bs.at[k - 1], br.at[k], exp=to_of(k)).wait_recv()

    seg_copy.wait_send()
    for i in range(1, n_exp):
        x_copy(i).wait_send()
        g_copy(i).wait_send()
        b_copy(i).wait_send()
    for d in range(1, n_dp):
        for block in range(n_exp):
            forward(d, block).wait_send()
        p_copy(d).wait_send()
    for c in range(chunks):
        out_copy(c).wait()
    own_back.wait()
    out_pick.wait()


def hand_on(pieces, back_ref, pick_ref, gin_ref, gx_out, gin_out, back_v, pick_v, gin_v, gx_v, sems):
    rows = gin_ref.shape[0] // pieces
    count, cap, width = back_ref.shape
    load_pick = pltpu.make_async_copy(pick_ref, pick_v, sems.at[2, 0])
    load_back = pltpu.make_async_copy(back_ref, back_v, sems.at[2, 1])
    store_x = pltpu.make_async_copy(gx_v, gx_out, sems.at[2, 2])
    loads, stores = [], []
    for p in range(pieces):
        at = pl.ds(p * rows, rows)
        loads.append(pltpu.make_async_copy(gin_ref.at[at], gin_v.at[at], sems.at[0, p]))
        stores.append(pltpu.make_async_copy(gin_v.at[at], gin_out.at[at], sems.at[1, p]))
    load_pick.start()
    load_back.start()
    for load in loads:
        load.start()
    load_pick.wait()
    load_back.wait()
    held = back_v[...].astype(F32).reshape(count * cap, width).astype(BF16)
    gx_v[...] = jnp.dot(pick_v[...], held, preferred_element_type=F32).astype(BF16)
    store_x.start()
    for load, store in zip(loads, stores):
        load.wait()
        store.start()
    for store in stores:
        store.wait()
    store_x.wait()


def body(saved_b, route_b, gate_b, grad_y_b, w_in, w_out):
    n_seg, n_dp, n_exp = lax.axis_size("segment"), lax.axis_size("dp"), lax.axis_size("expert")
    tok, width = saved_b.shape[1], saved_b.shape[2]
    hidden = w_in.shape[3]
    part = hidden // n_dp
    most = max(2, tok * 5 // (4 * n_exp))
    cap = -(-most // 8) * 8
    chunks = 4
    vmem = pl.BlockSpec(memory_space=pltpu.VMEM)
    hbm = pl.BlockSpec(memory_space=pl.ANY)
    dma = pltpu.SemaphoreType.DMA
    flops = 8 * n_exp * cap * width * hidden
    back, pick, grad_in = pl.pallas_call(
        functools.partial(kernel, (n_seg, n_dp, n_exp, cap, chunks)),
        out_shape=(
            jax.ShapeDtypeStruct((n_exp, cap, width), BF16),
            jax.ShapeDtypeStruct((tok, n_exp * cap), BF16),
            jax.ShapeDtypeStruct((width, part), BF16),
        ),
        in_specs=[vmem, vmem, hbm, hbm, hbm, hbm],
        out_specs=(hbm, hbm, hbm),
        scratch_shapes=[
            pltpu.VMEM((tok, width), BF16),
            pltpu.VMEM((tok, width), BF16),
            pltpu.VMEM((width, hidden), BF16),
            pltpu.VMEM((hidden, width), BF16),
            pltpu.VMEM((n_exp - 1, cap, width), BF16),
            pltpu.VMEM((n_exp - 1, cap, width), BF16),
            pltpu.VMEM((n_dp, n_exp, cap, width), BF16),
            pltpu.VMEM((n_exp, cap, width), BF16),
            pltpu.VMEM((n_exp, cap, hidden), F32),
            pltpu.VMEM((n_dp, n_exp, cap, part), BF16),
            pltpu.VMEM((n_dp, n_exp, cap, part), BF16),
            pltpu.VMEM((n_exp - 1, cap, width), BF16),
            pltpu.VMEM((cap, width), BF16),
            pltpu.VMEM((tok, n_exp * cap), BF16),
            pltpu.VMEM((width, part), BF16),
            dma((5,)),
            dma((1,)), dma((1,)),
            dma((n_exp,)), dma((n_exp,)),
            dma((n_exp,)), dma((n_exp,)),
            dma((n_dp, n_exp)), dma((n_dp, n_exp)),
            dma((n_dp,)), dma((n_dp,)),
            dma((n_exp,)), dma((n_exp,)),
            dma((chunks,)),
        ],
        compiler_params=pltpu.CompilerParams(
            collective_id=0, has_side_effects=True, vmem_limit_bytes=56 * 1024 * 1024
        ),
        cost_estimate=pl.CostEstimate(flops=flops, bytes_accessed=10 * 1024 * 1024, transcendentals=0),
    )(route_b.reshape(1, tok), gate_b.reshape(1, tok), saved_b, grad_y_b, w_in, w_out)
    pieces = 4
    grad_x, grad_in = pl.pallas_call(
        functools.partial(hand_on, pieces),
        out_shape=(
            jax.ShapeDtypeStruct((tok, width), BF16),
            jax.ShapeDtypeStruct((width, part), BF16),
        ),
        in_specs=[hbm, hbm, hbm],
        out_specs=(hbm, hbm),
        scratch_shapes=[
            pltpu.VMEM((n_exp, cap, width), BF16),
            pltpu.VMEM((tok, n_exp * cap), BF16),
            pltpu.VMEM((width, part), BF16),
            pltpu.VMEM((tok, width), BF16),
            dma((3, pieces)),
        ],
        compiler_params=pltpu.CompilerParams(vmem_limit_bytes=56 * 1024 * 1024),
    )(back, pick, grad_in)
    return (grad_x[None], grad_in[None, None])


def solution(mesh):
    return jax.shard_map(
        body,
        mesh=mesh,
        in_specs=(
            P("segment", ("dp", "expert"), None),
            P("segment", ("dp", "expert"), None),
            P("segment", ("dp", "expert"), None),
            P("segment", ("dp", "expert"), None),
            P("segment", "expert", None, None),
            P("segment", "expert", None, None),
        ),
        out_specs=(P("segment", ("dp", "expert"), None), P("segment", "expert", None, "dp")),
        check_vma=False,
    )
```

```python
import functools
import jax
import jax.numpy as jnp
from jax import lax
from jax.experimental import pallas as pl
from jax.experimental.pallas import tpu as pltpu
from jax.sharding import PartitionSpec as P

F32 = jnp.float32
BF16 = jnp.bfloat16


def kernel(
    sizes,
    route_ref, gate_ref, saved_hbm, gy_hbm, win_hbm, wout_hbm,
    back, pick_hbm, gin_hbm,
    saved_v, cot, win_v, wout_v, send_x, send_g, x_all, g_all, dsilu,
    gp_send, gp_all, ret, own_ret, pick, gin_v,
    loc, seg_s, seg_r, xs, xr, gs, gr, fs, fr, ps, pr, bs, br, outs,
):
    n_seg, n_dp, n_exp, cap, chunks = sizes
    me_s, me_d, me_z = lax.axis_index("segment"), lax.axis_index("dp"), lax.axis_index("expert")
    tok, width = saved_v.shape
    hidden = win_v.shape[1]
    part = hidden // n_dp
    step = width // chunks

    paired = n_exp & (n_exp - 1) == 0

    def flip(k):
        other, bit = me_z, 1
        while bit < n_exp:
            other = other + bit * (k // bit % 2) * (1 - 2 * (me_z // bit % 2))
            bit *= 2
        return other

    def to_of(k):
        return flip(k) if paired else lax.rem(me_z + k, n_exp)

    def from_of(k):
        return flip(k) if paired else lax.rem(me_z + n_exp - k, n_exp)

    half = max(1, n_exp // 2)
    inner = (me_z + half // 2) // half % 2

    def order(i, far_first):
        return 1 + lax.rem(i - 1 + far_first * (half - 1), max(1, n_exp - 1))

    def remote(src, dst, ss, rs, seg=None, dp=None, exp=None):
        dev = (
            me_s if seg is None else seg,
            me_d if dp is None else dp,
            me_z if exp is None else exp,
        )
        return pltpu.make_async_remote_copy(
            src_ref=src, dst_ref=dst, send_sem=ss, recv_sem=rs,
            device_id=dev, device_id_type=pl.DeviceIdType.MESH,
        )

    in_saved = pltpu.make_async_copy(saved_hbm.at[0], saved_v, loc.at[0])
    in_win = pltpu.make_async_copy(win_hbm.at[0, 0], win_v, loc.at[1])
    in_wout = pltpu.make_async_copy(wout_hbm.at[0, 0], wout_v, loc.at[2])
    in_saved.start()

    before_s = lax.rem(me_s + n_seg - 1, n_seg)
    after_s = lax.rem(me_s + 1, n_seg)
    barrier = pltpu.get_barrier_semaphore()
    peers = [(before_s, me_d, me_z), (after_s, me_d, me_z)]
    peers += [(me_s, lax.rem(me_d + d, n_dp), me_z) for d in range(1, n_dp)]
    peers += [(me_s, me_d, lax.rem(me_z + k, n_exp)) for k in range(1, n_exp)]
    for peer in peers:
        pl.semaphore_signal(barrier, inc=1, device_id=peer, device_id_type=pl.DeviceIdType.MESH)

    rows_t = lax.broadcasted_iota(jnp.int32, (tok, tok), 0)
    cols_t = lax.broadcasted_iota(jnp.int32, (tok, tok), 1)
    route = jnp.sum(jnp.where(rows_t == cols_t, route_ref[...], 0), axis=1, keepdims=True)
    gate = jnp.sum(jnp.where(rows_t == cols_t, gate_ref[...], 0.0), axis=1, keepdims=True)
    lanes = lax.broadcasted_iota(jnp.int32, (tok, 128), 1)
    onehot = (route == lanes).astype(F32)
    lower = (cols_t < rows_t).astype(BF16)
    ahead = jnp.dot(lower, onehot.astype(BF16), preferred_element_type=F32)
    rank = jnp.sum(ahead * onehot, axis=1, keepdims=True).astype(jnp.int32)
    pos_col = route * cap + rank
    pos_row = jnp.sum(jnp.where(rows_t == cols_t, pos_col, 0), axis=0, keepdims=True)

    def table(expert):
        slots = lax.broadcasted_iota(jnp.int32, (cap, tok), 0) + expert * cap
        return (slots == pos_row).astype(F32).astype(BF16)

    if paired:
        apart, bit = route * 0, 1
        while bit < n_exp:
            one, two = route // bit % 2, me_z // bit % 2
            apart = apart + bit * (one + two - 2 * one * two)
            bit *= 2
    else:
        apart = lax.rem(route + n_exp - me_z, n_exp)
    places = lax.broadcasted_iota(jnp.int32, (tok, n_exp * cap), 1)
    pick[...] = (places == apart * cap + rank).astype(F32).astype(BF16)
    out_pick = pltpu.make_async_copy(pick, pick_hbm, loc.at[4])
    out_pick.start()

    in_saved.wait()
    saved = saved_v[...]
    for i in range(1, n_exp):
        send_x[i - 1] = jnp.dot(table(to_of(i)), saved, preferred_element_type=F32).astype(BF16)

    pl.semaphore_wait(barrier, len(peers))
    seg_copy = remote(gy_hbm.at[0], cot, seg_s.at[0], seg_r.at[0], seg=before_s)

    def x_copy(i):
        return remote(send_x.at[i - 1], x_all.at[me_d, i], xs.at[i - 1], xr.at[i], exp=to_of(i))

    x_copy(order(1, inner)).start()
    seg_copy.start()
    for i in range(2, n_exp):
        x_copy(order(i, inner)).start()
    in_win.start()
    in_wout.start()
    x_all[me_d, 0] = jnp.dot(table(me_z), saved, preferred_element_type=F32).astype(BF16)

    def forward(d, block):
        return remote(
            x_all.at[me_d, block], x_all.at[me_d, block],
            fs.at[d - 1, block], fr.at[me_d, block], dp=lax.rem(me_d + d, n_dp),
        )

    for d in range(1, n_dp):
        forward(d, 0).start()

    seg_copy.wait_recv()
    scaled = (gate * cot[...].astype(F32)).astype(BF16)

    def g_copy(i):
        return remote(send_g.at[i - 1], g_all.at[i], gs.at[i - 1], gr.at[i], exp=to_of(i))

    for i in range(1, n_exp):
        send_g[i - 1] = jnp.dot(table(to_of(i)), scaled, preferred_element_type=F32).astype(BF16)
        g_copy(i).start()
    g_all[0] = jnp.dot(table(me_z), scaled, preferred_element_type=F32).astype(BF16)

    for i in range(1, n_exp):
        k = order(i, 1 - inner)
        remote(send_x.at[k - 1], x_all.at[me_d, k], xs.at[k - 1], xr.at[k], exp=from_of(k)).wait_recv()
        for d in range(1, n_dp):
            forward(d, k).start()

    in_win.wait()
    own_x = x_all[me_d].astype(F32).reshape(n_exp * cap, width).astype(BF16)
    pre = jnp.dot(own_x, win_v[...], preferred_element_type=F32)
    sigma = jax.nn.sigmoid(pre)
    dsilu[...] = (sigma * (1.0 + pre * (1.0 - sigma))).reshape(n_exp, cap, hidden)
    in_wout.wait()

    def g_wait(k):
        remote(send_g.at[k - 1], g_all.at[k], gs.at[k - 1], gr.at[k], exp=from_of(k)).wait_recv()

    def b_copy(k):
        return remote(ret.at[k - 1], back.at[k], bs.at[k - 1], br.at[k], exp=from_of(k))

    own_back = pltpu.make_async_copy(own_ret, back.at[0], loc.at[3])

    def expert_blocks(first, last):
        count = last - first
        rows = g_all[first:last].astype(F32).reshape(count * cap, width).astype(BF16)
        grad_h = lax.dot_general(
            rows, wout_v[...], (((1,), (1,)), ((), ())), preferred_element_type=F32
        )
        scale = dsilu[first:last].reshape(count * cap, hidden)
        grad_pre = (grad_h * scale).astype(BF16)
        grad_x = lax.dot_general(
            grad_pre, win_v[...], (((1,), (1,)), ((), ())), preferred_element_type=F32
        ).reshape(count, cap, width)
        for k in range(first, last):
            if k:
                ret[k - 1] = grad_x[k - first].astype(BF16)
                b_copy(k).start()
            else:
                own_ret[...] = grad_x[0].astype(BF16)
                own_back.start()
        wide = grad_pre.astype(F32).reshape(count, cap, hidden).astype(BF16)
        for j in range(n_dp):
            gp_send[j, first:last] = wide[:, :, j * part:(j + 1) * part]

    for k in range(1, half):
        g_wait(k)
    expert_blocks(0, half)
    for k in range(half, n_exp):
        g_wait(k)
        expert_blocks(k, k + 1)

    def p_copy(d):
        other = lax.rem(me_d + d, n_dp)
        return remote(gp_send.at[other], gp_all.at[me_d], ps.at[d - 1], pr.at[me_d], dp=other)

    for d in range(1, n_dp):
        p_copy(d).start()
    gp_all[me_d] = gp_send[me_d]

    for d in range(1, n_dp):
        other = lax.rem(me_d + n_dp - d, n_dp)
        for block in range(n_exp):
            remote(
                x_all.at[other, block], x_all.at[other, block],
                fs.at[d - 1, block], fr.at[other, block], dp=other,
            ).wait_recv()
        remote(gp_send.at[other], gp_all.at[other], ps.at[d - 1], pr.at[other], dp=other).wait_recv()

    all_gp = gp_all[...].astype(F32).reshape(n_dp * n_exp * cap, part).astype(BF16)

    def out_copy(c):
        rows = pl.ds(pl.multiple_of(c * step, step), step)
        return pltpu.make_async_copy(gin_v.at[rows], gin_hbm.at[rows], outs.at[c])

    def one_chunk(c, carry):
        at = pl.ds(pl.multiple_of(c * step, step), step)
        xs_c = x_all[:, :, :, at].astype(F32).reshape(n_dp * n_exp * cap, step).astype(BF16)
        gin_v[at, :] = lax.dot_general(
            xs_c, all_gp, (((0,), (0,)), ((), ())), preferred_element_type=F32
        ).astype(BF16)
        out_copy(c).start()
        return carry

    lax.fori_loop(0, chunks, one_chunk, 0)

    for k in range(1, n_exp):
        remote(ret.at[k - 1], back.at[k], bs.at[k - 1], br.at[k], exp=to_of(k)).wait_recv()

    seg_copy.wait_send()
    for i in range(1, n_exp):
        x_copy(i).wait_send()
        g_copy(i).wait_send()
        b_copy(i).wait_send()
    for d in range(1, n_dp):
        for block in range(n_exp):
            forward(d, block).wait_send()
        p_copy(d).wait_send()
    for c in range(chunks):
        out_copy(c).wait()
    own_back.wait()
    out_pick.wait()


def hand_on(pieces, back_ref, pick_ref, gin_ref, gx_out, gin_out, back_v, pick_v, gin_v, gx_v, sems):
    rows = gin_ref.shape[0] // pieces
    count, cap, width = back_ref.shape
    load_pick = pltpu.make_async_copy(pick_ref, pick_v, sems.at[2, 0])
    load_back = pltpu.make_async_copy(back_ref, back_v, sems.at[2, 1])
    store_x = pltpu.make_async_copy(gx_v, gx_out, sems.at[2, 2])
    loads, stores = [], []
    for p in range(pieces):
        at = pl.ds(p * rows, rows)
        loads.append(pltpu.make_async_copy(gin_ref.at[at], gin_v.at[at], sems.at[0, p]))
        stores.append(pltpu.make_async_copy(gin_v.at[at], gin_out.at[at], sems.at[1, p]))
    load_pick.start()
    load_back.start()
    for load in loads:
        load.start()
    load_pick.wait()
    load_back.wait()
    held = back_v[...].astype(F32).reshape(count * cap, width).astype(BF16)
    gx_v[...] = jnp.dot(pick_v[...], held, preferred_element_type=F32).astype(BF16)
    store_x.start()
    for load, store in zip(loads, stores):
        load.wait()
        store.start()
    for store in stores:
        store.wait()
    store_x.wait()


def body(saved_b, route_b, gate_b, grad_y_b, w_in, w_out):
    n_seg, n_dp, n_exp = lax.axis_size("segment"), lax.axis_size("dp"), lax.axis_size("expert")
    tok, width = saved_b.shape[1], saved_b.shape[2]
    hidden = w_in.shape[3]
    part = hidden // n_dp
    most = max(2, tok * 5 // (4 * n_exp))
    cap = -(-most // 8) * 8
    chunks = 4
    vmem = pl.BlockSpec(memory_space=pltpu.VMEM)
    hbm = pl.BlockSpec(memory_space=pl.ANY)
    dma = pltpu.SemaphoreType.DMA
    flops = 8 * n_exp * cap * width * hidden
    back, pick, grad_in = pl.pallas_call(
        functools.partial(kernel, (n_seg, n_dp, n_exp, cap, chunks)),
        out_shape=(
            jax.ShapeDtypeStruct((n_exp, cap, width), BF16),
            jax.ShapeDtypeStruct((tok, n_exp * cap), BF16),
            jax.ShapeDtypeStruct((width, part), BF16),
        ),
        in_specs=[vmem, vmem, hbm, hbm, hbm, hbm],
        out_specs=(hbm, hbm, hbm),
        scratch_shapes=[
            pltpu.VMEM((tok, width), BF16),
            pltpu.VMEM((tok, width), BF16),
            pltpu.VMEM((width, hidden), BF16),
            pltpu.VMEM((hidden, width), BF16),
            pltpu.VMEM((n_exp - 1, cap, width), BF16),
            pltpu.VMEM((n_exp - 1, cap, width), BF16),
            pltpu.VMEM((n_dp, n_exp, cap, width), BF16),
            pltpu.VMEM((n_exp, cap, width), BF16),
            pltpu.VMEM((n_exp, cap, hidden), F32),
            pltpu.VMEM((n_dp, n_exp, cap, part), BF16),
            pltpu.VMEM((n_dp, n_exp, cap, part), BF16),
            pltpu.VMEM((n_exp - 1, cap, width), BF16),
            pltpu.VMEM((cap, width), BF16),
            pltpu.VMEM((tok, n_exp * cap), BF16),
            pltpu.VMEM((width, part), BF16),
            dma((5,)),
            dma((1,)), dma((1,)),
            dma((n_exp,)), dma((n_exp,)),
            dma((n_exp,)), dma((n_exp,)),
            dma((n_dp, n_exp)), dma((n_dp, n_exp)),
            dma((n_dp,)), dma((n_dp,)),
            dma((n_exp,)), dma((n_exp,)),
            dma((chunks,)),
        ],
        compiler_params=pltpu.CompilerParams(
            collective_id=0, has_side_effects=True, vmem_limit_bytes=56 * 1024 * 1024
        ),
        cost_estimate=pl.CostEstimate(flops=flops, bytes_accessed=10 * 1024 * 1024, transcendentals=0),
    )(route_b.reshape(1, tok), gate_b.reshape(1, tok), saved_b, grad_y_b, w_in, w_out)
    pieces = 4
    grad_x, grad_in = pl.pallas_call(
        functools.partial(hand_on, pieces),
        out_shape=(
            jax.ShapeDtypeStruct((tok, width), BF16),
            jax.ShapeDtypeStruct((width, part), BF16),
        ),
        in_specs=[hbm, hbm, hbm],
        out_specs=(hbm, hbm),
        scratch_shapes=[
            pltpu.VMEM((n_exp, cap, width), BF16),
            pltpu.VMEM((tok, n_exp * cap), BF16),
            pltpu.VMEM((width, part), BF16),
            pltpu.VMEM((tok, width), BF16),
            dma((3, pieces)),
        ],
        compiler_params=pltpu.CompilerParams(vmem_limit_bytes=56 * 1024 * 1024),
    )(back, pick, grad_in)
    return (grad_x[None], grad_in[None, None])


def solution(mesh):
    return jax.shard_map(
        body,
        mesh=mesh,
        in_specs=(
            P("segment", ("dp", "expert"), None),
            P("segment", ("dp", "expert"), None),
            P("segment", ("dp", "expert"), None),
            P("segment", ("dp", "expert"), None),
            P("segment", "expert", None, None),
            P("segment", "expert", None, None),
        ),
        out_specs=(P("segment", ("dp", "expert"), None), P("segment", "expert", None, "dp")),
        check_vma=False,
    )
```

```python
import functools
import jax
import jax.numpy as jnp
from jax import lax
from jax.experimental import pallas as pl
from jax.experimental.pallas import tpu as pltpu
from jax.sharding import PartitionSpec as P

F32 = jnp.float32
BF16 = jnp.bfloat16


def kernel(
    sizes,
    route_ref, gate_ref, saved_hbm, gy_hbm, win_hbm, wout_hbm,
    back, pick_hbm, gin_hbm,
    saved_v, cot, win_v, wout_v, send_x, send_g, x_all, g_all, dsilu,
    gp_send, gp_all, ret, own_ret, pick, gin_v,
    loc, seg_s, seg_r, xs, xr, gs, gr, fs, fr, ps, pr, bs, br, outs,
):
    n_seg, n_dp, n_exp, cap, chunks = sizes
    me_s, me_d, me_z = lax.axis_index("segment"), lax.axis_index("dp"), lax.axis_index("expert")
    tok, width = saved_v.shape
    hidden = win_v.shape[1]
    part = hidden // n_dp
    step = width // chunks

    paired = n_exp & (n_exp - 1) == 0

    def flip(k):
        other, bit = me_z, 1
        while bit < n_exp:
            other = other + bit * (k // bit % 2) * (1 - 2 * (me_z // bit % 2))
            bit *= 2
        return other

    def to_of(k):
        return flip(k) if paired else lax.rem(me_z + k, n_exp)

    def from_of(k):
        return flip(k) if paired else lax.rem(me_z + n_exp - k, n_exp)

    half = max(1, n_exp // 2)
    inner = (me_z + half // 2) // half % 2

    near, far = list(range(1, half)), list(range(half, n_exp))

    def by_place(ends, inners):
        return [end + inner * (mid - end) for end, mid in zip(ends, inners)]

    order_x = by_place(near + far, far[::-1] + near)
    order_far = by_place(far, far[::-1])
    order_g = near + order_far

    def remote(src, dst, ss, rs, seg=None, dp=None, exp=None):
        dev = (
            me_s if seg is None else seg,
            me_d if dp is None else dp,
            me_z if exp is None else exp,
        )
        return pltpu.make_async_remote_copy(
            src_ref=src, dst_ref=dst, send_sem=ss, recv_sem=rs,
            device_id=dev, device_id_type=pl.DeviceIdType.MESH,
        )

    in_saved = pltpu.make_async_copy(saved_hbm.at[0], saved_v, loc.at[0])
    in_win = pltpu.make_async_copy(win_hbm.at[0, 0], win_v, loc.at[1])
    in_wout = pltpu.make_async_copy(wout_hbm.at[0, 0], wout_v, loc.at[2])
    in_saved.start()

    before_s = lax.rem(me_s + n_seg - 1, n_seg)
    after_s = lax.rem(me_s + 1, n_seg)
    barrier = pltpu.get_barrier_semaphore()
    peers = [(before_s, me_d, me_z), (after_s, me_d, me_z)]
    peers += [(me_s, lax.rem(me_d + d, n_dp), me_z) for d in range(1, n_dp)]
    peers += [(me_s, me_d, lax.rem(me_z + k, n_exp)) for k in range(1, n_exp)]
    for peer in peers:
        pl.semaphore_signal(barrier, inc=1, device_id=peer, device_id_type=pl.DeviceIdType.MESH)

    rows_t = lax.broadcasted_iota(jnp.int32, (tok, tok), 0)
    cols_t = lax.broadcasted_iota(jnp.int32, (tok, tok), 1)
    route = jnp.sum(jnp.where(rows_t == cols_t, route_ref[...], 0), axis=1, keepdims=True)
    gate = jnp.sum(jnp.where(rows_t == cols_t, gate_ref[...], 0.0), axis=1, keepdims=True)
    lanes = lax.broadcasted_iota(jnp.int32, (tok, 128), 1)
    onehot = (route == lanes).astype(F32)
    lower = (cols_t < rows_t).astype(BF16)
    ahead = jnp.dot(lower, onehot.astype(BF16), preferred_element_type=F32)
    rank = jnp.sum(ahead * onehot, axis=1, keepdims=True).astype(jnp.int32)
    pos_col = route * cap + rank
    pos_row = jnp.sum(jnp.where(rows_t == cols_t, pos_col, 0), axis=0, keepdims=True)

    def table(expert):
        slots = lax.broadcasted_iota(jnp.int32, (cap, tok), 0) + expert * cap
        return (slots == pos_row).astype(F32).astype(BF16)

    if paired:
        apart, bit = route * 0, 1
        while bit < n_exp:
            one, two = route // bit % 2, me_z // bit % 2
            apart = apart + bit * (one + two - 2 * one * two)
            bit *= 2
    else:
        apart = lax.rem(route + n_exp - me_z, n_exp)
    places = lax.broadcasted_iota(jnp.int32, (tok, n_exp * cap), 1)
    pick[...] = (places == apart * cap + rank).astype(F32).astype(BF16)
    out_pick = pltpu.make_async_copy(pick, pick_hbm, loc.at[4])
    out_pick.start()

    in_saved.wait()
    saved = saved_v[...]
    for i in range(1, n_exp):
        send_x[i - 1] = jnp.dot(table(to_of(i)), saved, preferred_element_type=F32).astype(BF16)

    pl.semaphore_wait(barrier, len(peers))
    seg_copy = remote(gy_hbm.at[0], cot, seg_s.at[0], seg_r.at[0], seg=before_s)

    def x_copy(i):
        return remote(send_x.at[i - 1], x_all.at[me_d, i], xs.at[i - 1], xr.at[i], exp=to_of(i))

    seg_copy.start()
    for k in order_x:
        x_copy(k).start()
    in_win.start()
    in_wout.start()
    x_all[me_d, 0] = jnp.dot(table(me_z), saved, preferred_element_type=F32).astype(BF16)

    def forward(d, block):
        return remote(
            x_all.at[me_d, block], x_all.at[me_d, block],
            fs.at[d - 1, block], fr.at[me_d, block], dp=lax.rem(me_d + d, n_dp),
        )

    for d in range(1, n_dp):
        forward(d, 0).start()

    seg_copy.wait_recv()
    scaled = (gate * cot[...].astype(F32)).astype(BF16)

    def g_copy(i):
        return remote(send_g.at[i - 1], g_all.at[i], gs.at[i - 1], gr.at[i], exp=to_of(i))

    for k in order_g:
        send_g[k - 1] = jnp.dot(table(to_of(k)), scaled, preferred_element_type=F32).astype(BF16)
        g_copy(k).start()
    g_all[0] = jnp.dot(table(me_z), scaled, preferred_element_type=F32).astype(BF16)

    for k in order_g:
        remote(send_x.at[k - 1], x_all.at[me_d, k], xs.at[k - 1], xr.at[k], exp=from_of(k)).wait_recv()
        for d in range(1, n_dp):
            forward(d, k).start()

    in_win.wait()
    own_x = x_all[me_d].astype(F32).reshape(n_exp * cap, width).astype(BF16)
    pre = jnp.dot(own_x, win_v[...], preferred_element_type=F32)
    sigma = jax.nn.sigmoid(pre)
    dsilu[...] = (sigma * (1.0 + pre * (1.0 - sigma))).reshape(n_exp, cap, hidden)
    in_wout.wait()

    def g_wait(k):
        remote(send_g.at[k - 1], g_all.at[k], gs.at[k - 1], gr.at[k], exp=from_of(k)).wait_recv()

    def b_copy(k):
        return remote(ret.at[k - 1], back.at[k], bs.at[k - 1], br.at[k], exp=from_of(k))

    own_back = pltpu.make_async_copy(own_ret, back.at[0], loc.at[3])

    def expert_rows(rows, scale):
        grad_h = lax.dot_general(
            rows, wout_v[...], (((1,), (1,)), ((), ())), preferred_element_type=F32
        )
        grad_pre = (grad_h * scale).astype(BF16)
        return grad_pre, lax.dot_general(
            grad_pre, win_v[...], (((1,), (1,)), ((), ())), preferred_element_type=F32
        )

    def near_blocks():
        rows = g_all[:half].astype(F32).reshape(half * cap, width).astype(BF16)
        grad_pre, grad_x = expert_rows(rows, dsilu[:half].reshape(half * cap, hidden))
        grad_x = grad_x.reshape(half, cap, width)
        for k in near:
            ret[k - 1] = grad_x[k].astype(BF16)
            b_copy(k).start()
        own_ret[...] = grad_x[0].astype(BF16)
        own_back.start()
        wide = grad_pre.astype(F32).reshape(half, cap, hidden).astype(BF16)
        for j in range(n_dp):
            gp_send[j, :half] = wide[:, :, j * part:(j + 1) * part]

    def far_block(k):
        grad_pre, grad_x = expert_rows(g_all[k], dsilu[k])
        ret[k - 1] = grad_x.astype(BF16)
        b_copy(k).start()
        for j in range(n_dp):
            gp_send[j, k] = grad_pre[:, j * part:(j + 1) * part]

    for k in range(1, half):
        g_wait(k)
    near_blocks()
    for k in order_far:
        g_wait(k)
        far_block(k)

    def p_copy(d):
        other = lax.rem(me_d + d, n_dp)
        return remote(gp_send.at[other], gp_all.at[me_d], ps.at[d - 1], pr.at[me_d], dp=other)

    for d in range(1, n_dp):
        p_copy(d).start()
    gp_all[me_d] = gp_send[me_d]

    for d in range(1, n_dp):
        other = lax.rem(me_d + n_dp - d, n_dp)
        for block in range(n_exp):
            remote(
                x_all.at[other, block], x_all.at[other, block],
                fs.at[d - 1, block], fr.at[other, block], dp=other,
            ).wait_recv()
        remote(gp_send.at[other], gp_all.at[other], ps.at[d - 1], pr.at[other], dp=other).wait_recv()

    all_gp = gp_all[...].astype(F32).reshape(n_dp * n_exp * cap, part).astype(BF16)

    def out_copy(c):
        rows = pl.ds(pl.multiple_of(c * step, step), step)
        return pltpu.make_async_copy(gin_v.at[rows], gin_hbm.at[rows], outs.at[c])

    def one_chunk(c, carry):
        at = pl.ds(pl.multiple_of(c * step, step), step)
        xs_c = x_all[:, :, :, at].astype(F32).reshape(n_dp * n_exp * cap, step).astype(BF16)
        gin_v[at, :] = lax.dot_general(
            xs_c, all_gp, (((0,), (0,)), ((), ())), preferred_element_type=F32
        ).astype(BF16)
        out_copy(c).start()
        return carry

    lax.fori_loop(0, chunks, one_chunk, 0)

    for k in range(1, n_exp):
        remote(ret.at[k - 1], back.at[k], bs.at[k - 1], br.at[k], exp=to_of(k)).wait_recv()

    seg_copy.wait_send()
    for i in range(1, n_exp):
        x_copy(i).wait_send()
        g_copy(i).wait_send()
        b_copy(i).wait_send()
    for d in range(1, n_dp):
        for block in range(n_exp):
            forward(d, block).wait_send()
        p_copy(d).wait_send()
    for c in range(chunks):
        out_copy(c).wait()
    own_back.wait()
    out_pick.wait()


def hand_on(pieces, back_ref, pick_ref, gin_ref, gx_out, gin_out, back_v, pick_v, gin_v, gx_v, sems):
    rows = gin_ref.shape[0] // pieces
    count, cap, width = back_ref.shape
    load_pick = pltpu.make_async_copy(pick_ref, pick_v, sems.at[2, 0])
    load_back = pltpu.make_async_copy(back_ref, back_v, sems.at[2, 1])
    store_x = pltpu.make_async_copy(gx_v, gx_out, sems.at[2, 2])
    loads, stores = [], []
    for p in range(pieces):
        at = pl.ds(p * rows, rows)
        loads.append(pltpu.make_async_copy(gin_ref.at[at], gin_v.at[at], sems.at[0, p]))
        stores.append(pltpu.make_async_copy(gin_v.at[at], gin_out.at[at], sems.at[1, p]))
    load_pick.start()
    load_back.start()
    for load in loads:
        load.start()
    load_pick.wait()
    load_back.wait()
    held = back_v[...].astype(F32).reshape(count * cap, width).astype(BF16)
    gx_v[...] = jnp.dot(pick_v[...], held, preferred_element_type=F32).astype(BF16)
    store_x.start()
    for load, store in zip(loads, stores):
        load.wait()
        store.start()
    for store in stores:
        store.wait()
    store_x.wait()


def body(saved_b, route_b, gate_b, grad_y_b, w_in, w_out):
    n_seg, n_dp, n_exp = lax.axis_size("segment"), lax.axis_size("dp"), lax.axis_size("expert")
    tok, width = saved_b.shape[1], saved_b.shape[2]
    hidden = w_in.shape[3]
    part = hidden // n_dp
    most = max(2, tok * 5 // (4 * n_exp))
    cap = -(-most // 8) * 8
    chunks = 4
    vmem = pl.BlockSpec(memory_space=pltpu.VMEM)
    hbm = pl.BlockSpec(memory_space=pl.ANY)
    dma = pltpu.SemaphoreType.DMA
    flops = 8 * n_exp * cap * width * hidden
    back, pick, grad_in = pl.pallas_call(
        functools.partial(kernel, (n_seg, n_dp, n_exp, cap, chunks)),
        out_shape=(
            jax.ShapeDtypeStruct((n_exp, cap, width), BF16),
            jax.ShapeDtypeStruct((tok, n_exp * cap), BF16),
            jax.ShapeDtypeStruct((width, part), BF16),
        ),
        in_specs=[vmem, vmem, hbm, hbm, hbm, hbm],
        out_specs=(hbm, hbm, hbm),
        scratch_shapes=[
            pltpu.VMEM((tok, width), BF16),
            pltpu.VMEM((tok, width), BF16),
            pltpu.VMEM((width, hidden), BF16),
            pltpu.VMEM((hidden, width), BF16),
            pltpu.VMEM((n_exp - 1, cap, width), BF16),
            pltpu.VMEM((n_exp - 1, cap, width), BF16),
            pltpu.VMEM((n_dp, n_exp, cap, width), BF16),
            pltpu.VMEM((n_exp, cap, width), BF16),
            pltpu.VMEM((n_exp, cap, hidden), F32),
            pltpu.VMEM((n_dp, n_exp, cap, part), BF16),
            pltpu.VMEM((n_dp, n_exp, cap, part), BF16),
            pltpu.VMEM((n_exp - 1, cap, width), BF16),
            pltpu.VMEM((cap, width), BF16),
            pltpu.VMEM((tok, n_exp * cap), BF16),
            pltpu.VMEM((width, part), BF16),
            dma((5,)),
            dma((1,)), dma((1,)),
            dma((n_exp,)), dma((n_exp,)),
            dma((n_exp,)), dma((n_exp,)),
            dma((n_dp, n_exp)), dma((n_dp, n_exp)),
            dma((n_dp,)), dma((n_dp,)),
            dma((n_exp,)), dma((n_exp,)),
            dma((chunks,)),
        ],
        compiler_params=pltpu.CompilerParams(
            collective_id=0, has_side_effects=True, vmem_limit_bytes=56 * 1024 * 1024
        ),
        cost_estimate=pl.CostEstimate(flops=flops, bytes_accessed=10 * 1024 * 1024, transcendentals=0),
    )(route_b.reshape(1, tok), gate_b.reshape(1, tok), saved_b, grad_y_b, w_in, w_out)
    pieces = 4
    grad_x, grad_in = pl.pallas_call(
        functools.partial(hand_on, pieces),
        out_shape=(
            jax.ShapeDtypeStruct((tok, width), BF16),
            jax.ShapeDtypeStruct((width, part), BF16),
        ),
        in_specs=[hbm, hbm, hbm],
        out_specs=(hbm, hbm),
        scratch_shapes=[
            pltpu.VMEM((n_exp, cap, width), BF16),
            pltpu.VMEM((tok, n_exp * cap), BF16),
            pltpu.VMEM((width, part), BF16),
            pltpu.VMEM((tok, width), BF16),
            dma((3, pieces)),
        ],
        compiler_params=pltpu.CompilerParams(vmem_limit_bytes=56 * 1024 * 1024),
    )(back, pick, grad_in)
    return (grad_x[None], grad_in[None, None])


def solution(mesh):
    return jax.shard_map(
        body,
        mesh=mesh,
        in_specs=(
            P("segment", ("dp", "expert"), None),
            P("segment", ("dp", "expert"), None),
            P("segment", ("dp", "expert"), None),
            P("segment", ("dp", "expert"), None),
            P("segment", "expert", None, None),
            P("segment", "expert", None, None),
        ),
        out_specs=(P("segment", ("dp", "expert"), None), P("segment", "expert", None, "dp")),
        check_vma=False,
    )
```

```python
import functools
import jax
import jax.numpy as jnp
from jax import lax
from jax.experimental import pallas as pl
from jax.experimental.pallas import tpu as pltpu
from jax.sharding import PartitionSpec as P

F32 = jnp.float32
BF16 = jnp.bfloat16


def kernel(
    sizes,
    route_ref, gate_ref, saved_hbm, gy_hbm, win_hbm, wout_hbm,
    back, pick_hbm, gin_hbm,
    saved_v, cot, win_v, wout_v, send_x, send_g, x_all, g_all, dsilu,
    gp_send, gp_all, ret, own_ret, pick, gin_v,
    loc, seg_s, seg_r, xs, xr, gs, gr, fs, fr, ps, pr, bs, br, outs,
):
    n_seg, n_dp, n_exp, cap, chunks = sizes
    me_s, me_d, me_z = lax.axis_index("segment"), lax.axis_index("dp"), lax.axis_index("expert")
    tok, width = saved_v.shape
    hidden = win_v.shape[1]
    part = hidden // n_dp
    step = width // chunks

    paired = n_exp & (n_exp - 1) == 0

    def flip(k):
        other, bit = me_z, 1
        while bit < n_exp:
            other = other + bit * (k // bit % 2) * (1 - 2 * (me_z // bit % 2))
            bit *= 2
        return other

    def to_of(k):
        return flip(k) if paired else lax.rem(me_z + k, n_exp)

    def from_of(k):
        return flip(k) if paired else lax.rem(me_z + n_exp - k, n_exp)

    half = max(1, n_exp // 2)
    inner = (me_z + half // 2) // half % 2

    near, far = list(range(1, half)), list(range(half, n_exp))

    lower = inner * (1 - me_z // half)
    turned = [lower * (b - a) for a, b in zip(far, far[::-1])]
    order_far = [k + t for k, t in zip(far, turned)]
    order_x = [
        end + inner * (mid - end) + t
        for end, mid, t in zip(near + far, far + near, turned + [0] * len(near))
    ]
    order_g = near + order_far

    def remote(src, dst, ss, rs, seg=None, dp=None, exp=None):
        dev = (
            me_s if seg is None else seg,
            me_d if dp is None else dp,
            me_z if exp is None else exp,
        )
        return pltpu.make_async_remote_copy(
            src_ref=src, dst_ref=dst, send_sem=ss, recv_sem=rs,
            device_id=dev, device_id_type=pl.DeviceIdType.MESH,
        )

    in_saved = pltpu.make_async_copy(saved_hbm.at[0], saved_v, loc.at[0])
    in_win = pltpu.make_async_copy(win_hbm.at[0, 0], win_v, loc.at[1])
    in_wout = pltpu.make_async_copy(wout_hbm.at[0, 0], wout_v, loc.at[2])
    in_saved.start()

    before_s = lax.rem(me_s + n_seg - 1, n_seg)
    after_s = lax.rem(me_s + 1, n_seg)
    barrier = pltpu.get_barrier_semaphore()
    peers = [(before_s, me_d, me_z), (after_s, me_d, me_z)]
    peers += [(me_s, lax.rem(me_d + d, n_dp), me_z) for d in range(1, n_dp)]
    peers += [(me_s, me_d, lax.rem(me_z + k, n_exp)) for k in range(1, n_exp)]
    for peer in peers:
        pl.semaphore_signal(barrier, inc=1, device_id=peer, device_id_type=pl.DeviceIdType.MESH)

    rows_t = lax.broadcasted_iota(jnp.int32, (tok, tok), 0)
    cols_t = lax.broadcasted_iota(jnp.int32, (tok, tok), 1)
    route = jnp.sum(jnp.where(rows_t == cols_t, route_ref[...], 0), axis=1, keepdims=True)
    gate = jnp.sum(jnp.where(rows_t == cols_t, gate_ref[...], 0.0), axis=1, keepdims=True)
    lanes = lax.broadcasted_iota(jnp.int32, (tok, 128), 1)
    onehot = (route == lanes).astype(F32)
    lower = (cols_t < rows_t).astype(BF16)
    ahead = jnp.dot(lower, onehot.astype(BF16), preferred_element_type=F32)
    rank = jnp.sum(ahead * onehot, axis=1, keepdims=True).astype(jnp.int32)
    pos_col = route * cap + rank
    pos_row = jnp.sum(jnp.where(rows_t == cols_t, pos_col, 0), axis=0, keepdims=True)

    def table(expert):
        slots = lax.broadcasted_iota(jnp.int32, (cap, tok), 0) + expert * cap
        return (slots == pos_row).astype(F32).astype(BF16)

    if paired:
        apart, bit = route * 0, 1
        while bit < n_exp:
            one, two = route // bit % 2, me_z // bit % 2
            apart = apart + bit * (one + two - 2 * one * two)
            bit *= 2
    else:
        apart = lax.rem(route + n_exp - me_z, n_exp)
    places = lax.broadcasted_iota(jnp.int32, (tok, n_exp * cap), 1)
    pick[...] = (places == apart * cap + rank).astype(F32).astype(BF16)
    out_pick = pltpu.make_async_copy(pick, pick_hbm, loc.at[4])
    out_pick.start()

    in_saved.wait()
    saved = saved_v[...]
    for i in range(1, n_exp):
        send_x[i - 1] = jnp.dot(table(to_of(i)), saved, preferred_element_type=F32).astype(BF16)

    pl.semaphore_wait(barrier, len(peers))
    seg_copy = remote(gy_hbm.at[0], cot, seg_s.at[0], seg_r.at[0], seg=before_s)

    def x_copy(i):
        return remote(send_x.at[i - 1], x_all.at[me_d, i], xs.at[i - 1], xr.at[i], exp=to_of(i))

    seg_copy.start()
    for k in order_x:
        x_copy(k).start()
    in_win.start()
    in_wout.start()
    x_all[me_d, 0] = jnp.dot(table(me_z), saved, preferred_element_type=F32).astype(BF16)

    def forward(d, block):
        return remote(
            x_all.at[me_d, block], x_all.at[me_d, block],
            fs.at[d - 1, block], fr.at[me_d, block], dp=lax.rem(me_d + d, n_dp),
        )

    for d in range(1, n_dp):
        forward(d, 0).start()

    seg_copy.wait_recv()
    scaled = (gate * cot[...].astype(F32)).astype(BF16)

    def g_copy(i):
        return remote(send_g.at[i - 1], g_all.at[i], gs.at[i - 1], gr.at[i], exp=to_of(i))

    for k in order_g:
        send_g[k - 1] = jnp.dot(table(to_of(k)), scaled, preferred_element_type=F32).astype(BF16)
        g_copy(k).start()
    g_all[0] = jnp.dot(table(me_z), scaled, preferred_element_type=F32).astype(BF16)

    for k in order_g:
        remote(send_x.at[k - 1], x_all.at[me_d, k], xs.at[k - 1], xr.at[k], exp=from_of(k)).wait_recv()
        for d in range(1, n_dp):
            forward(d, k).start()

    in_win.wait()
    own_x = x_all[me_d].astype(F32).reshape(n_exp * cap, width).astype(BF16)
    pre = jnp.dot(own_x, win_v[...], preferred_element_type=F32)
    sigma = jax.nn.sigmoid(pre)
    dsilu[...] = (sigma * (1.0 + pre * (1.0 - sigma))).reshape(n_exp, cap, hidden)
    in_wout.wait()

    def g_wait(k):
        remote(send_g.at[k - 1], g_all.at[k], gs.at[k - 1], gr.at[k], exp=from_of(k)).wait_recv()

    def b_copy(k):
        return remote(ret.at[k - 1], back.at[k], bs.at[k - 1], br.at[k], exp=from_of(k))

    own_back = pltpu.make_async_copy(own_ret, back.at[0], loc.at[3])

    def expert_rows(rows, scale):
        grad_h = lax.dot_general(
            rows, wout_v[...], (((1,), (1,)), ((), ())), preferred_element_type=F32
        )
        grad_pre = (grad_h * scale).astype(BF16)
        return grad_pre, lax.dot_general(
            grad_pre, win_v[...], (((1,), (1,)), ((), ())), preferred_element_type=F32
        )

    def near_blocks():
        rows = g_all[:half].astype(F32).reshape(half * cap, width).astype(BF16)
        grad_pre, grad_x = expert_rows(rows, dsilu[:half].reshape(half * cap, hidden))
        grad_x = grad_x.reshape(half, cap, width)
        for k in near:
            ret[k - 1] = grad_x[k].astype(BF16)
            b_copy(k).start()
        own_ret[...] = grad_x[0].astype(BF16)
        own_back.start()
        wide = grad_pre.astype(F32).reshape(half, cap, hidden).astype(BF16)
        for j in range(n_dp):
            gp_send[j, :half] = wide[:, :, j * part:(j + 1) * part]

    def far_block(k):
        grad_pre, grad_x = expert_rows(g_all[k], dsilu[k])
        ret[k - 1] = grad_x.astype(BF16)
        b_copy(k).start()
        for j in range(n_dp):
            gp_send[j, k] = grad_pre[:, j * part:(j + 1) * part]

    for k in range(1, half):
        g_wait(k)
    near_blocks()
    for k in order_far:
        g_wait(k)
        far_block(k)

    def p_copy(d):
        other = lax.rem(me_d + d, n_dp)
        return remote(gp_send.at[other], gp_all.at[me_d], ps.at[d - 1], pr.at[me_d], dp=other)

    for d in range(1, n_dp):
        p_copy(d).start()
    gp_all[me_d] = gp_send[me_d]

    for d in range(1, n_dp):
        other = lax.rem(me_d + n_dp - d, n_dp)
        for block in range(n_exp):
            remote(
                x_all.at[other, block], x_all.at[other, block],
                fs.at[d - 1, block], fr.at[other, block], dp=other,
            ).wait_recv()
        remote(gp_send.at[other], gp_all.at[other], ps.at[d - 1], pr.at[other], dp=other).wait_recv()

    all_gp = gp_all[...].astype(F32).reshape(n_dp * n_exp * cap, part).astype(BF16)

    def out_copy(c):
        rows = pl.ds(pl.multiple_of(c * step, step), step)
        return pltpu.make_async_copy(gin_v.at[rows], gin_hbm.at[rows], outs.at[c])

    def one_chunk(c, carry):
        at = pl.ds(pl.multiple_of(c * step, step), step)
        xs_c = x_all[:, :, :, at].astype(F32).reshape(n_dp * n_exp * cap, step).astype(BF16)
        gin_v[at, :] = lax.dot_general(
            xs_c, all_gp, (((0,), (0,)), ((), ())), preferred_element_type=F32
        ).astype(BF16)
        out_copy(c).start()
        return carry

    lax.fori_loop(0, chunks, one_chunk, 0)

    for k in range(1, n_exp):
        remote(ret.at[k - 1], back.at[k], bs.at[k - 1], br.at[k], exp=to_of(k)).wait_recv()

    seg_copy.wait_send()
    for i in range(1, n_exp):
        x_copy(i).wait_send()
        g_copy(i).wait_send()
        b_copy(i).wait_send()
    for d in range(1, n_dp):
        for block in range(n_exp):
            forward(d, block).wait_send()
        p_copy(d).wait_send()
    for c in range(chunks):
        out_copy(c).wait()
    own_back.wait()
    out_pick.wait()


def hand_on(pieces, back_ref, pick_ref, gin_ref, gx_out, gin_out, back_v, pick_v, gin_v, gx_v, sems):
    rows = gin_ref.shape[0] // pieces
    count, cap, width = back_ref.shape
    load_pick = pltpu.make_async_copy(pick_ref, pick_v, sems.at[2, 0])
    load_back = pltpu.make_async_copy(back_ref, back_v, sems.at[2, 1])
    store_x = pltpu.make_async_copy(gx_v, gx_out, sems.at[2, 2])
    loads, stores = [], []
    for p in range(pieces):
        at = pl.ds(p * rows, rows)
        loads.append(pltpu.make_async_copy(gin_ref.at[at], gin_v.at[at], sems.at[0, p]))
        stores.append(pltpu.make_async_copy(gin_v.at[at], gin_out.at[at], sems.at[1, p]))
    load_pick.start()
    load_back.start()
    for load in loads:
        load.start()
    load_pick.wait()
    load_back.wait()
    held = back_v[...].astype(F32).reshape(count * cap, width).astype(BF16)
    gx_v[...] = jnp.dot(pick_v[...], held, preferred_element_type=F32).astype(BF16)
    store_x.start()
    for load, store in zip(loads, stores):
        load.wait()
        store.start()
    for store in stores:
        store.wait()
    store_x.wait()


def body(saved_b, route_b, gate_b, grad_y_b, w_in, w_out):
    n_seg, n_dp, n_exp = lax.axis_size("segment"), lax.axis_size("dp"), lax.axis_size("expert")
    tok, width = saved_b.shape[1], saved_b.shape[2]
    hidden = w_in.shape[3]
    part = hidden // n_dp
    most = max(2, tok * 5 // (4 * n_exp))
    cap = -(-most // 8) * 8
    chunks = 4
    vmem = pl.BlockSpec(memory_space=pltpu.VMEM)
    hbm = pl.BlockSpec(memory_space=pl.ANY)
    dma = pltpu.SemaphoreType.DMA
    flops = 8 * n_exp * cap * width * hidden
    back, pick, grad_in = pl.pallas_call(
        functools.partial(kernel, (n_seg, n_dp, n_exp, cap, chunks)),
        out_shape=(
            jax.ShapeDtypeStruct((n_exp, cap, width), BF16),
            jax.ShapeDtypeStruct((tok, n_exp * cap), BF16),
            jax.ShapeDtypeStruct((width, part), BF16),
        ),
        in_specs=[vmem, vmem, hbm, hbm, hbm, hbm],
        out_specs=(hbm, hbm, hbm),
        scratch_shapes=[
            pltpu.VMEM((tok, width), BF16),
            pltpu.VMEM((tok, width), BF16),
            pltpu.VMEM((width, hidden), BF16),
            pltpu.VMEM((hidden, width), BF16),
            pltpu.VMEM((n_exp - 1, cap, width), BF16),
            pltpu.VMEM((n_exp - 1, cap, width), BF16),
            pltpu.VMEM((n_dp, n_exp, cap, width), BF16),
            pltpu.VMEM((n_exp, cap, width), BF16),
            pltpu.VMEM((n_exp, cap, hidden), F32),
            pltpu.VMEM((n_dp, n_exp, cap, part), BF16),
            pltpu.VMEM((n_dp, n_exp, cap, part), BF16),
            pltpu.VMEM((n_exp - 1, cap, width), BF16),
            pltpu.VMEM((cap, width), BF16),
            pltpu.VMEM((tok, n_exp * cap), BF16),
            pltpu.VMEM((width, part), BF16),
            dma((5,)),
            dma((1,)), dma((1,)),
            dma((n_exp,)), dma((n_exp,)),
            dma((n_exp,)), dma((n_exp,)),
            dma((n_dp, n_exp)), dma((n_dp, n_exp)),
            dma((n_dp,)), dma((n_dp,)),
            dma((n_exp,)), dma((n_exp,)),
            dma((chunks,)),
        ],
        compiler_params=pltpu.CompilerParams(
            collective_id=0, has_side_effects=True, vmem_limit_bytes=56 * 1024 * 1024
        ),
        cost_estimate=pl.CostEstimate(flops=flops, bytes_accessed=10 * 1024 * 1024, transcendentals=0),
    )(route_b.reshape(1, tok), gate_b.reshape(1, tok), saved_b, grad_y_b, w_in, w_out)
    pieces = 4
    grad_x, grad_in = pl.pallas_call(
        functools.partial(hand_on, pieces),
        out_shape=(
            jax.ShapeDtypeStruct((tok, width), BF16),
            jax.ShapeDtypeStruct((width, part), BF16),
        ),
        in_specs=[hbm, hbm, hbm],
        out_specs=(hbm, hbm),
        scratch_shapes=[
            pltpu.VMEM((n_exp, cap, width), BF16),
            pltpu.VMEM((tok, n_exp * cap), BF16),
            pltpu.VMEM((width, part), BF16),
            pltpu.VMEM((tok, width), BF16),
            dma((3, pieces)),
        ],
        compiler_params=pltpu.CompilerParams(vmem_limit_bytes=56 * 1024 * 1024),
    )(back, pick, grad_in)
    return (grad_x[None], grad_in[None, None])


def solution(mesh):
    return jax.shard_map(
        body,
        mesh=mesh,
        in_specs=(
            P("segment", ("dp", "expert"), None),
            P("segment", ("dp", "expert"), None),
            P("segment", ("dp", "expert"), None),
            P("segment", ("dp", "expert"), None),
            P("segment", "expert", None, None),
            P("segment", "expert", None, None),
        ),
        out_specs=(P("segment", ("dp", "expert"), None), P("segment", "expert", None, "dp")),
        check_vma=False,
    )
```
